32 devices in a mesh: row: 4 (over y, x), col: 8 (over z, core).
Axes of the slice: x: 2, y: 2, z: 4, core: 2. Of those that a mesh axis runs over, the one named last changes fastest.
Arguments:
- latent: bfloat16 [128, 40960], P('row', 'col'), may hold values from -6 to 6
- tile_reach: int32 [4, 8, 4], replicated, may hold values from 1 to 4
- first_weight: bfloat16 [3, 3, 320, 320], replicated, may hold values from -0.109375 to 0.109375
- first_bias: float32 [320], replicated, may hold values from -3 to 3
- second_weight: bfloat16 [3, 3, 320, 320], replicated, may hold values from -0.109375 to 0.109375
- second_bias: float32 [320], replicated, may hold values from -3 to 3
- proj_weight: bfloat16 [320, 512], replicated, may hold values from -0.3125 to 0.3125
- upper_weight: bfloat16 [3, 3, 512, 512], replicated, may hold values from -0.09375 to 0.09375
- upper_bias: float32 [512], replicated, may hold values from -3 to 3
- lower_weight: bfloat16 [3, 3, 512, 512], replicated, may hold values from -0.09375 to 0.09375
- lower_bias: float32 [512], replicated, may hold values from -3 to 3
Outputs:
- decoded: bfloat16 [256, 256, 512], P(('row', 'col'))
The draws below stay inside these ranges and needn't reach their ends.
All inputs are finite; a program needn't handle non-finite values.
Results may differ from the reference program's by a relative error of at most 0.0065.
Values may be sent and summed in bfloat16 or wider, within the bound.
No kernel may reach another device: no remote copies, remote signals or barrier semaphores. Data moves between devices by JAX's collectives and lax.ppermute only.
A program may use at most 64 MiB of HBM per device.

```python
import jax
import jax.numpy as jnp
from jax import lax

C = 320
DC = 512
CH = 32
CW = 16
MARGIN = 4
NH = 128
NW = 128
N_ROW = 4
N_COL = 8


def plant(drawn, own_key, low, top_value):
    shape = drawn.shape
    spot = [jax.random.randint(jax.random.fold_in(own_key, axis), (), 0, shape[axis]) for axis in range(len(shape))]
    drawn = drawn.at[tuple(spot)].set(low)
    longest = shape.index(max(shape))
    spot[longest] = (spot[longest] + 1) % shape[longest]
    return drawn.at[tuple(spot)].set(top_value)


def block_levels(rng, dims, cuts, low, largest):
    def one(axis_at, blocks):
        steps = jax.random.uniform(jax.random.fold_in(jax.random.fold_in(rng, 6), axis_at), (blocks,), jnp.float32, low / len(cuts), largest / len(cuts))
        return jnp.repeat(jnp.exp(steps), dims[axis_at] // blocks).reshape((-1,) + (1,) * (len(dims) - axis_at - 1))

    gain = one(*cuts[0])
    for cut in cuts[1:]:
        gain = gain * one(*cut)
    return gain


def gaussian(stream_key, extent, spread, reach, split=(), kind=jnp.bfloat16):
    entries = jax.random.normal(stream_key, extent, jnp.float32) * spread
    if len(split) > 0:
        entries = block_levels(stream_key, extent, split, -0.22, 0.18) * entries
    return jnp.clip(entries, min=-reach, max=reach).astype(kind)


def setup_inputs(seed: int = 0) -> dict:
    streams_of = jax.random.split(jax.random.key(seed), 12)
    latent = gaussian(streams_of[0], (NH, NW * C), 1.0, 6.0, ((0, 4), (1, 8)))
    tile_reach = plant(jax.random.randint(streams_of[1], (N_ROW, N_COL, 4), 1, MARGIN + 1), jax.random.fold_in(streams_of[1], 1), 1, MARGIN).astype(jnp.int32)
    first_weight = gaussian(streams_of[2], (3, 3, C, C), (9 * C) ** -0.5, 0.109375)
    first_bias = gaussian(streams_of[3], (C,), 0.5, 3.0, (), jnp.float32)
    second_weight = gaussian(streams_of[4], (3, 3, C, C), (9 * C) ** -0.5, 0.109375)
    second_bias = gaussian(streams_of[5], (C,), 0.5, 3.0, (), jnp.float32)
    proj_weight = gaussian(streams_of[6], (C, DC), C ** -0.5, 0.3125)
    upper_weight = gaussian(streams_of[7], (3, 3, DC, DC), (9 * DC) ** -0.5, 0.09375)
    upper_bias = gaussian(streams_of[8], (DC,), 0.5, 3.0, (), jnp.float32)
    lower_weight = gaussian(streams_of[9], (3, 3, DC, DC), (9 * DC) ** -0.5, 0.09375)
    lower_bias = gaussian(streams_of[10], (DC,), 0.5, 3.0, (), jnp.float32)
    return dict(latent=latent, tile_reach=tile_reach, first_weight=first_weight, first_bias=first_bias, second_weight=second_weight, second_bias=second_bias, proj_weight=proj_weight, upper_weight=upper_weight, upper_bias=upper_bias, lower_weight=lower_weight, lower_bias=lower_bias)


def convolve(inputs, weight, padding):
    return lax.conv_general_dilated(inputs[None], weight, (1, 1), padding, dimension_numbers=("NHWC", "HWIO", "NHWC"), preferred_element_type=jnp.float32)[0]


def tile_block(window, window_mask, first_weight, first_bias, second_weight, second_bias):
    mask_three = window_mask[:, :, None]
    masked = window * mask_three.astype(window.dtype)
    active = (jax.nn.silu(convolve(masked, first_weight, "SAME") + first_bias) * mask_three).astype(jnp.bfloat16)
    summed = masked.astype(jnp.float32) + convolve(active, second_weight, "SAME") + second_bias
    return (summed * mask_three).astype(jnp.bfloat16)


def reference(latent, tile_reach, first_weight, first_bias, second_weight, second_bias, proj_weight, upper_weight, upper_bias, lower_weight, lower_bias):
    canvas_start = latent.reshape(NH, NW, C)
    padded = jnp.pad(canvas_start, ((MARGIN, MARGIN), (MARGIN, MARGIN), (0, 0)))
    span_rows = CH + 2 * MARGIN
    span_cols = CW + 2 * MARGIN
    offset_rows = jnp.arange(span_rows, dtype=jnp.int32) - MARGIN
    offset_cols = jnp.arange(span_cols, dtype=jnp.int32) - MARGIN

    def visit(carry, flat):
        sums, counts = carry
        row_id = flat // N_COL
        col_id = flat % N_COL
        reach_row = tile_reach[row_id, col_id]
        glob_rows = row_id * CH + offset_rows
        glob_cols = col_id * CW + offset_cols
        rows_ok = (glob_rows >= row_id * CH - reach_row[0]) & (glob_rows < (row_id + 1) * CH + reach_row[1]) & (glob_rows >= 0) & (glob_rows < NH)
        cols_ok = (glob_cols >= col_id * CW - reach_row[2]) & (glob_cols < (col_id + 1) * CW + reach_row[3]) & (glob_cols >= 0) & (glob_cols < NW)
        window_mask = (rows_ok[:, None] & cols_ok[None, :]).astype(jnp.float32)
        start_row = (row_id * CH).astype(jnp.int32)
        start_col = (col_id * CW).astype(jnp.int32)
        zero = jnp.zeros((), jnp.int32)
        window = lax.dynamic_slice(padded, (start_row, start_col, zero), (span_rows, span_cols, C))
        output = tile_block(window, window_mask, first_weight, first_bias, second_weight, second_bias)
        old_sum = lax.dynamic_slice(sums, (start_row, start_col, zero), (span_rows, span_cols, C))
        sums = lax.dynamic_update_slice(sums, old_sum + output.astype(jnp.float32), (start_row, start_col, zero))
        old_count = lax.dynamic_slice(counts, (start_row, start_col), (span_rows, span_cols))
        counts = lax.dynamic_update_slice(counts, old_count + window_mask, (start_row, start_col))
        return (sums, counts), None

    init = (jnp.zeros((NH + 2 * MARGIN, NW + 2 * MARGIN, C), jnp.float32), jnp.zeros((NH + 2 * MARGIN, NW + 2 * MARGIN), jnp.float32))
    (sums, counts), _ = lax.scan(visit, init, jnp.arange(N_ROW * N_COL, dtype=jnp.int32))
    blend = sums[MARGIN:-MARGIN, MARGIN:-MARGIN]
    canvas = (blend / counts[MARGIN:-MARGIN, MARGIN:-MARGIN, None]).astype(jnp.bfloat16)
    hidden = jnp.dot(canvas.reshape(NH * NW, C), proj_weight, preferred_element_type=jnp.float32).astype(jnp.bfloat16).reshape(NH, NW, DC)
    upsampled = jnp.repeat(jnp.repeat(hidden, 2, axis=0), 2, axis=1)
    active = jax.nn.silu(convolve(upsampled, upper_weight, "SAME") + upper_bias).astype(jnp.bfloat16)
    decoded = convolve(active, lower_weight, "SAME") + lower_bias + upsampled.astype(jnp.float32)
    return decoded.astype(jnp.bfloat16)
```

```python
import jax
import jax.numpy as jnp
from jax import lax
from jax.sharding import PartitionSpec as P

MARGIN = 4
HALO = 3


def convolve(inputs, weight, padding):
    return lax.conv_general_dilated(
        inputs,
        weight,
        (1, 1),
        padding,
        dimension_numbers=("NHWC", "HWIO", "NHWC"),
        preferred_element_type=jnp.float32,
    )


def shifted_rows(rows, hops, n_all, width):
    own = rows.shape[0]
    above, below = [], []
    left = width
    for hop in range(1, hops + 1):
        take = min(own, left)
        above.insert(
            0,
            lax.ppermute(
                rows[own - take :], ("row", "col"), [(i, i + hop) for i in range(n_all - hop)]
            ),
        )
        below.append(
            lax.ppermute(
                rows[:take], ("row", "col"), [(i + hop, i) for i in range(n_all - hop)]
            )
        )
        left -= take
    return above, below


def on_device(
    latent,
    tile_reach,
    first_weight,
    first_bias,
    second_weight,
    second_bias,
    proj_weight,
    upper_weight,
    upper_bias,
    lower_weight,
    lower_bias,
):
    chans = first_weight.shape[2]
    tile_rows = latent.shape[0]
    tile_cols = latent.shape[1] // chans
    n_row = lax.axis_size("row")
    n_col = lax.axis_size("col")
    row_id = lax.axis_index("row")
    col_id = lax.axis_index("col")
    own = tile_rows // n_col
    width = n_col * tile_cols
    total_rows = tile_rows * n_row
    span = tile_cols + 2 * MARGIN
    first_row = row_id * tile_rows + col_id * own

    moved = lax.all_to_all(
        latent.reshape(n_col, own, tile_cols * chans), "col", split_axis=0, concat_axis=0
    )
    rows = moved.reshape(n_col, own, tile_cols, chans).transpose(1, 0, 2, 3)
    hops = -(-HALO // own)
    above, below = shifted_rows(rows, hops, n_row * n_col, HALO)
    tall = jnp.concatenate(above + [rows] + below, axis=0)
    side = jnp.pad(tall, ((0, 0), (1, 1), (0, 0), (0, 0)))
    window = jnp.concatenate(
        [side[:, :-2, -MARGIN:], tall, side[:, 2:, :MARGIN]], axis=2
    )

    upper_band = col_id < n_col // 2
    other = jnp.where(upper_band, row_id - 1, row_id + 1)
    bands = jnp.stack([row_id, other])
    band_ok = (bands >= 0) & (bands < n_row)
    reach = tile_reach[jnp.clip(bands, 0, n_row - 1)]
    glob_rows = first_row - HALO + jnp.arange(own + 2 * HALO, dtype=jnp.int32)
    glob_cols = (
        jnp.arange(n_col, dtype=jnp.int32)[:, None] * tile_cols
        - MARGIN
        + jnp.arange(span, dtype=jnp.int32)[None, :]
    )
    col_lo = jnp.arange(n_col, dtype=jnp.int32) * tile_cols
    rows_ok = (
        (glob_rows[None, :, None] >= (bands[:, None] * tile_rows - reach[:, :, 0])[:, None, :])
        & (glob_rows[None, :, None] < ((bands[:, None] + 1) * tile_rows + reach[:, :, 1])[:, None, :])
        & (glob_rows >= 0)[None, :, None]
        & (glob_rows < total_rows)[None, :, None]
        & band_ok[:, None, None]
    )
    cols_ok = (
        (glob_cols[None] >= (col_lo[None, :] - reach[:, :, 2])[:, :, None])
        & (glob_cols[None] < (col_lo[None, :] + tile_cols + reach[:, :, 3])[:, :, None])
        & (glob_cols >= 0)[None]
        & (glob_cols < width)[None]
    )
    mask = (rows_ok[:, :, :, None] & cols_ok[:, None, :, :]).astype(jnp.float32)
    mask = mask.transpose(0, 2, 1, 3).reshape(2 * n_col, own + 2 * HALO, span, 1)
    tiles = window.transpose(1, 0, 2, 3)
    tiles = jnp.concatenate([tiles, tiles], axis=0)
    masked = tiles * mask.astype(tiles.dtype)
    no_rows = ((0, 0), (1, 1))
    active = (
        jax.nn.silu(convolve(masked, first_weight, no_rows) + first_bias) * mask[:, 1:-1]
    ).astype(jnp.bfloat16)
    output = (
        (
            masked[:, 2:-2].astype(jnp.float32)
            + convolve(active, second_weight, no_rows)
            + second_bias
        )
        * mask[:, 2:-2]
    ).astype(jnp.bfloat16)

    def fold(values):
        values = values.astype(jnp.float32)
        values = values.reshape((2, n_col) + values.shape[1:])
        values = (values[0] + values[1]).transpose(1, 0, 2, 3)
        middle = values[:, :, MARGIN:-MARGIN]
        pads = ((0, 0), (1, 1), (0, 0), (0, 0))
        after = jnp.pad(values[:, :, -MARGIN:], pads)[:, :-2]
        before = jnp.pad(values[:, :, :MARGIN], pads)[:, 2:]
        gap = ((0, 0), (0, 0))
        return (
            middle
            + jnp.pad(after, gap + ((0, tile_cols - MARGIN), (0, 0)))
            + jnp.pad(before, gap + ((tile_cols - MARGIN, 0), (0, 0)))
        )

    counts = fold(mask[:, 2:-2])
    canvas = jnp.where(counts > 0, fold(output) / jnp.maximum(counts, 1.0), 0.0)
    canvas = canvas.astype(jnp.bfloat16)
    hidden = jnp.dot(
        canvas.reshape(-1, chans), proj_weight, preferred_element_type=jnp.float32
    ).astype(jnp.bfloat16)
    hidden = hidden.reshape(own + 2, width, proj_weight.shape[1])
    upsampled = jnp.repeat(jnp.repeat(hidden, 2, axis=0), 2, axis=1)
    out_rows = 2 * first_row - 1 + jnp.arange(2 * own + 2, dtype=jnp.int32)
    keep = ((out_rows >= 0) & (out_rows < 2 * total_rows)).astype(jnp.float32)
    decoder_act = (
        jax.nn.silu(convolve(upsampled[None], upper_weight, no_rows)[0] + upper_bias)
        * keep[:, None, None]
    ).astype(jnp.bfloat16)
    decoded = (
        convolve(decoder_act[None], lower_weight, no_rows)[0]
        + lower_bias
        + upsampled[2:-2].astype(jnp.float32)
    )
    return decoded.astype(jnp.bfloat16)


def solution(mesh):
    in_specs = (P("row", "col"), P(), P(), P(), P(), P(), P(), P(), P(), P(), P())
    out_specs = P(("row", "col"), None, None)
    return jax.shard_map(
        on_device, mesh=mesh, in_specs=in_specs, out_specs=out_specs, check_vma=False
    )
```

```python
import jax
import jax.numpy as jnp
from jax import lax
from jax.experimental import pallas as pl
from jax.experimental.pallas import tpu as pltpu
from jax.sharding import PartitionSpec as P

BF = jnp.bfloat16
F32 = jnp.float32
MARGIN = 4
HALO = 3
VMEM_LIMIT = 62 * 1024 * 1024


def silu(v):
    return v / (1.0 + jnp.exp(-v))


def tap_kernel(w_ref, main_ref, rest_ref):
    chans = w_ref.shape[2]
    main = chans // 128 * 128
    rest = chans - main
    depth = main_ref.shape[0] // 3
    main_ref[...] = jnp.zeros_like(main_ref)
    rest_ref[...] = jnp.zeros_like(rest_ref)
    for dy in range(3):
        for dx in range(3):
            main_ref[dy * depth + dx * main : dy * depth + dx * main + main, :] = w_ref[dy, dx, :main, :main]
            at = 3 * main + dx * rest
            main_ref[dy * depth + at : dy * depth + at + rest, :] = w_ref[dy, dx, main:, :main]
    for dx in range(3):
        for lo, n, at in ((0, main, dx * main), (main, rest, 3 * main + dx * rest)):
            tails = [w_ref[dy, dx, lo : lo + n, main:].astype(F32) for dy in range(3)]
            rest_ref[at : at + n, :128] = jnp.concatenate(tails[:2], axis=1).astype(BF)
            rest_ref[at : at + n, 128 : 128 + rest] = tails[2].astype(BF)


def setup_kernel(w1_ref, w2_ref, m1_ref, r1_ref, m2_ref, r2_ref):
    tap_kernel(w1_ref, m1_ref, r1_ref)
    tap_kernel(w2_ref, m2_ref, r2_ref)


def setup_call(w1, w2):
    chans = w1.shape[2]
    main = chans // 128 * 128
    rest = chans - main
    assert 2 * rest == 128
    depth = 3 * main + 4 * rest
    taps = [jax.ShapeDtypeStruct((3 * depth, main), BF), jax.ShapeDtypeStruct((depth, 256), BF)]
    return pl.pallas_call(
        setup_kernel,
        out_shape=taps + taps,
        compiler_params=pltpu.CompilerParams(vmem_limit_bytes=VMEM_LIMIT),
        cost_estimate=pl.CostEstimate(flops=0, bytes_accessed=8 << 20, transcendentals=0),
    )(w1, w2)


def put_cells(main_ref, rest_ref, r, v, main):
    span = v.shape[0]
    main_ref[r, pl.ds(1, span)] = v[:, :, :main].astype(BF)
    rest = v[:, :, main:]
    none = jnp.zeros((1,) + rest.shape[1:], F32)
    before = jnp.concatenate([none, rest[:-1]], axis=0)
    after = jnp.concatenate([rest[1:], none], axis=0)
    rest_ref[r, :, :, :128] = (before + pltpu.roll(rest, 64, 2)).astype(BF)
    rest_ref[r, :, :, 128:] = after.astype(BF)


def conv_group(main_ref, rest_ref, w_main, w_rest, start, rows):
    span, slots = rest_ref.shape[1:3]
    main = main_ref.shape[3]
    size = rows * span * slots
    parts = []
    for dy in range(3):
        for dx in range(3):
            parts.append(main_ref[pl.ds(start + dy, rows), pl.ds(dx, span)].reshape(size, main))
        parts.append(rest_ref[pl.ds(start + dy, rows)].reshape(size, 256))
    big = jnp.dot(jnp.concatenate(parts, axis=1), w_main[...], preferred_element_type=F32)
    size = (rows + 2) * span * slots
    parts = [main_ref[pl.ds(start, rows + 2), pl.ds(dx, span)].reshape(size, main) for dx in range(3)]
    parts.append(rest_ref[pl.ds(start, rows + 2)].reshape(size, 256))
    part = jnp.dot(jnp.concatenate(parts, axis=1), w_rest[...], preferred_element_type=F32)
    part = part.reshape(rows + 2, span, slots, 256)
    rest = part[:-2, :, :, :128] + pltpu.roll(part[1:-1, :, :, :128], 64, 3) + part[2:, :, :, 128:]
    return big.reshape(rows, span, slots, main), rest


def tile_body(geom, chans, tall, bounds_ref, m1, r1, b1_ref, m2, r2, b2_ref, canvas, xm, xr, am, ar, cells_ref, beside):
    n_row, n_col, tile_rows, tile_cols, own = geom
    slots = 2 * n_col
    span = tile_cols + 2 * MARGIN
    main = chans // 128 * 128
    lanes = main + 128
    rows_x = own + 2 * HALO
    width = n_col * tile_cols
    live = (lax.broadcasted_iota(jnp.int32, (1, 1, 128), 2) < chans - main).astype(F32)
    cell = lax.broadcasted_iota(jnp.int32, (span, slots, 128), 0)
    cols_ok = ((cell >= bounds_ref[2]) & (cell < bounds_ref[3])).astype(F32)
    xm[...] = jnp.zeros_like(xm)
    am[...] = jnp.zeros_like(am)

    def mask_of(r):
        row = jnp.zeros((slots, 128), jnp.int32) + r
        rows_ok = ((row >= bounds_ref[0]) & (row < bounds_ref[1])).astype(F32)
        return cols_ok * rows_ok

    def wide(m):
        return jnp.concatenate([m] * (lanes // 128), axis=2)

    r = 0
    for piece in tall:
        for k in range(piece.shape[0]):
            cols = []
            for c in range(tile_cols):
                lo = c * chans
                off = lo % 128
                v = piece[k, :, lo - off : lo - off + lanes].astype(F32)
                if off:
                    v = pltpu.roll(v, lanes - off, 1)
                cols.append(v)
            cells_ref[...] = jnp.stack(cols, axis=0)
            v = cells_ref[...]
            v = jnp.concatenate([v[:, :, :main], v[:, :, main:] * live], axis=2)
            v = jnp.concatenate(
                [pltpu.roll(v[-MARGIN:], 1, 1), v, pltpu.roll(v[:MARGIN], n_col - 1, 1)], axis=0)
            v = jnp.concatenate([v, v], axis=1)
            put_cells(xm, xr, r, v * wide(mask_of(r)), main)
            r += 1

    group1 = (rows_x - 2) // 2
    def first(g, carry):
        beside[0](g)
        big, rest = conv_group(xm, xr, m1, r1, g * group1, group1)
        for i in range(group1):
            a = g * group1 + i
            v = jnp.concatenate([big[i], rest[i] * live], axis=2) + b1_ref[...]
            put_cells(am, ar, a, silu(v) * wide(mask_of(a + 1)), main)
        return carry
    lax.fori_loop(0, 2, first, 0)

    group2 = (rows_x - 4) // 2
    def second(g, carry):
        beside[1](g)
        big, rest = conv_group(am, ar, m2, r2, g * group2, group2)
        for i in range(group2):
            a = g * group2 + i
            v = jnp.concatenate([big[i], rest[i] * live], axis=2) + b2_ref[...]
            x_rest = pltpu.roll(xr[a + 2, :, :, :128].astype(F32), 64, 2) * live
            x = jnp.concatenate([xm[a + 2, pl.ds(1, span)].astype(F32), x_rest], axis=2)
            mask = mask_of(a + 2)
            y = ((v + x) * wide(mask)).astype(BF).astype(F32)

            def fold(u):
                u = u[:, :n_col] + u[:, n_col:]
                mid = u[MARGIN:-MARGIN]
                return jnp.concatenate(
                    [
                        mid[:MARGIN] + pltpu.roll(u[-MARGIN:], 1, 1),
                        mid[MARGIN:-MARGIN],
                        mid[-MARGIN:] + pltpu.roll(u[:MARGIN], n_col - 1, 1),
                    ],
                    axis=0,
                )

            count = fold(mask)
            blend = fold(y) * wide(jnp.where(count > 0, 1.0 / jnp.maximum(count, 1.0), 0.0))
            for c in range(tile_cols):
                for lane in range(lanes // 128):
                    canvas[lane, pl.ds(a * width + c, n_col, stride=tile_cols), :] = blend[c, :, lane * 128 : lane * 128 + 128]
        return carry
    lax.fori_loop(0, 2, second, 0)


def tile_scratch(geom, chans):
    n_row, n_col, tile_rows, tile_cols, own = geom
    slots = 2 * n_col
    span = tile_cols + 2 * MARGIN
    main = chans // 128 * 128
    rows_x = own + 2 * HALO
    return [
        pltpu.VMEM((main // 128 + 1, (own + 2) * n_col * tile_cols, 128), F32),
        pltpu.VMEM((rows_x, span + 2, slots, main), BF),
        pltpu.VMEM((rows_x, span, slots, 256), BF),
        pltpu.VMEM((rows_x - 2, span + 2, slots, main), BF),
        pltpu.VMEM((rows_x - 2, span, slots, 256), BF),
        pltpu.VMEM((tile_cols, n_col, main + 128), F32),
    ]


def phase_part(w, out, k0, kn):
    ks = pl.ds(k0, kn)
    depth = w.shape[1]
    x = [[w[3 * dy + dx, ks, :].astype(F32) for dx in range(3)] for dy in range(3)]
    rowed = (
        (x[0], [a + b for a, b in zip(x[1], x[2])]),
        ([a + b for a, b in zip(x[0], x[1])], x[2]),
    )
    for p in range(2):
        for tap in range(2):
            u = rowed[p][tap]
            at = 2 * tap * depth + k0
            out[0, p, pl.ds(at, kn), :] = u[0].astype(BF)
            out[0, p, pl.ds(at + depth, kn), :] = (u[1] + u[2]).astype(BF)
            out[1, p, pl.ds(at, kn), :] = (u[0] + u[1]).astype(BF)
            out[1, p, pl.ds(at + depth, kn), :] = u[2].astype(BF)


def pair_part(w, out, k0, kn):
    ks = pl.ds(k0, kn)
    for dy in range(3):
        ends = 0.5 * (w[3 * dy, ks, :].astype(F32) + w[3 * dy + 2, ks, :].astype(F32))
        mid = 0.5 * w[3 * dy + 1, ks, :].astype(F32)
        w[3 * dy + 1, ks, :] = (ends + mid).astype(BF)
        out[dy, ks, :] = (ends - mid).astype(BF)


def decoder_body(
    keep, canvas, proj_ref, ub_ref, lb_ref, out_ref, left, hid, right, comps, edge, zipped,
    upper_v, lower_raw, pair_v,
):
    rows, width, dc = hid.shape
    steps = rows - 1
    own = rows - 2
    chans = proj_ref.shape[0]
    main = chans // 128 * 128

    edge[...] = jnp.zeros_like(edge)

    def hidden_row(r, carry):
        at = pl.ds(pl.multiple_of(r * width, width), width)
        x = jnp.concatenate([canvas[lane, at, :] for lane in range(main // 128)], axis=1).astype(BF)
        rest = canvas[main // 128, at, :].astype(BF)[:, : chans - main]
        h = jnp.dot(x, proj_ref[:main, :], preferred_element_type=F32)
        h = h + jnp.dot(rest, proj_ref[main:, :], preferred_element_type=F32)
        h = h.astype(BF)
        hid[r] = h
        edge[0, pl.ds(8, width), :] = h.astype(F32)
        left[r] = edge[0, pl.ds(7, width), :].astype(BF)
        right[r] = edge[0, pl.ds(9, width), :].astype(BF)
        return carry

    lax.fori_loop(0, rows, hidden_row, 0)

    def up_step(p, carry):
        acts = []
        for side, srcs in ((0, (left, hid)), (1, (hid, right))):
            lhs = jnp.concatenate(
                [src[pl.ds(i, steps)].reshape(steps * width, dc) for i in range(2) for src in srcs], axis=1
            )
            v = jnp.dot(lhs, upper_v[side, p], preferred_element_type=F32)
            acts.append(silu(v + ub_ref[...]).reshape(steps, width, dc))
        for k in range(steps):
            scale = 1.0
            if k == 0:
                scale = jnp.where(p == 1, keep[0], 1.0)
            if k == steps - 1:
                scale = jnp.where(p == 0, keep[1], 1.0)
            e = (acts[0][k] * scale).astype(BF).astype(F32)
            o = (acts[1][k] * scale).astype(BF).astype(F32)
            edge[0, pl.ds(8, width), :] = o
            edge[1, pl.ds(8, width), :] = e
            at = 2 * k + 1 - p
            comps[0, at] = (edge[0, pl.ds(7, width), :] - o).astype(BF)
            comps[1, at] = (e + o).astype(BF)
            comps[2, at] = (o - e).astype(BF)
            comps[3, at] = (e - edge[1, pl.ds(9, width), :]).astype(BF)
        return carry

    lax.fori_loop(0, 2, up_step, 0)

    group = max(own, 1)

    def low_step(n, carry):
        start = n * group
        prods = []
        for i in range(4):
            total = None
            for dy in range(3):
                lhs = comps[i, pl.ds(start + dy, group)].reshape(group * width, dc)
                rhs = pair_v[dy] if i == 2 else lower_raw[3 * dy + (0, 1, 0, 2)[i]]
                v = jnp.dot(lhs, rhs, preferred_element_type=F32)
                total = v if total is None else total + v
            prods.append(total)
        both = (prods[0] + prods[1] + prods[2], prods[1] - prods[2] - prods[3])
        for g in range(group):
            base = hid[1 + lax.div(start + g, 2)].astype(F32) + lb_ref[...]
            for side in range(2):
                v = both[side][g * width : (g + 1) * width] + base
                for lane in range(dc // 128):
                    zipped[lane, pl.ds(g * 2 * width + side, width, stride=2), :] = v[:, lane * 128 : lane * 128 + 128]
            for lane in range(dc // 128):
                out_ref[start + g, :, pl.ds(lane * 128, 128)] = zipped[lane, pl.ds(g * 2 * width, 2 * width), :].astype(BF)
        return carry

    lax.fori_loop(0, 2 * own // group, low_step, 0)


def main_kernel(
    geom, chans, n_tall, ids_ref, bounds_ref, m1, r1, m2, r2, bias_ref, proj_ref, upper_ref, lower_ref, *refs
):
    n_row, n_col, tile_rows, tile_cols, own = geom
    tall, refs = refs[:n_tall], refs[n_tall:]
    (out_ref, canvas, xm, xr, am, ar, cells_ref, left, hid, right, comps, edge, zipped,
     upper_raw, upper_v, lower_raw, pair_v, sems) = refs
    upper_copy = pltpu.make_async_copy(upper_ref, upper_raw, sems.at[0])
    lower_copy = pltpu.make_async_copy(lower_ref, lower_raw, sems.at[1])
    upper_copy.start()
    lower_copy.start()
    first_row = ids_ref[0] * tile_rows + ids_ref[1] * own
    keep = (
        jnp.where(first_row > 0, 1.0, 0.0),
        jnp.where(first_row + own < n_row * tile_rows, 1.0, 0.0),
    )
    lanes = chans // 128 * 128 + 128
    bias1, bias2 = bias_ref.at[pl.ds(0, 1), pl.ds(0, lanes)], bias_ref.at[pl.ds(1, 1), pl.ds(0, lanes)]
    part = upper_raw.shape[1] // 4

    def beside_first(g):
        @pl.when(g == 0)
        def _():
            upper_copy.wait()
        phase_part(upper_raw, upper_v, pl.multiple_of(g * part, part), part)

    def beside_second(g):
        @pl.when(g == 0)
        def _():
            lower_copy.wait()
        phase_part(upper_raw, upper_v, pl.multiple_of((g + 2) * part, part), part)
        pair_part(lower_raw, pair_v, pl.multiple_of(2 * g * part, 2 * part), 2 * part)

    tile_body(
        geom, chans, tall, bounds_ref, m1, r1, bias1, m2, r2, bias2, canvas, xm, xr, am, ar, cells_ref,
        (beside_first, beside_second),
    )
    decoder_body(
        keep, canvas, proj_ref, bias_ref.at[pl.ds(2, 1)], bias_ref.at[pl.ds(3, 1)], out_ref,
        left, hid, right, comps, edge, zipped, upper_v, lower_raw, pair_v,
    )


def main_call(geom, ids, tall, bounds, m1, r1, m2, r2, biases, proj, upper, lower, chans):
    n_row, n_col, tile_rows, tile_cols, own = geom
    width = n_col * tile_cols
    rows = own + 2
    dc = proj.shape[1]
    vm = pl.BlockSpec(memory_space=pltpu.VMEM)
    anyspace = pl.BlockSpec(memory_space=pl.ANY)

    def kernel(*refs):
        main_kernel(geom, chans, len(tall), *refs)

    return pl.pallas_call(
        kernel,
        out_shape=jax.ShapeDtypeStruct((2 * own, 2 * width, dc), BF),
        in_specs=[pl.BlockSpec(memory_space=pltpu.SMEM)] + [vm] * 7 + [anyspace] * 2 + [vm] * len(tall),
        out_specs=vm,
        scratch_shapes=tile_scratch(geom, chans)
        + [
            pltpu.VMEM((rows, width, dc), BF),
            pltpu.VMEM((rows, width, dc), BF),
            pltpu.VMEM((rows, width, dc), BF),
            pltpu.VMEM((4, 2 * own + 2, width, dc), BF),
            pltpu.VMEM((2, width + 16, dc), F32),
            pltpu.VMEM((dc // 128, 2 * own * width, 128), F32),
            pltpu.VMEM(upper.shape, BF),
            pltpu.VMEM((2, 2, 4 * dc, dc), BF),
            pltpu.VMEM(lower.shape, BF),
            pltpu.VMEM((3, dc, dc), BF),
            pltpu.SemaphoreType.DMA((2,)),
        ],
        compiler_params=pltpu.CompilerParams(vmem_limit_bytes=VMEM_LIMIT),
        cost_estimate=pl.CostEstimate(flops=25_000_000_000, bytes_accessed=20 << 20, transcendentals=0),
    )(ids, bounds, m1, r1, m2, r2, biases, proj, upper, lower, *tall)


def tile_bounds(tile_reach, row_id, col_id, n_row, n_col, tile_rows, tile_cols, own):
    first_row = row_id * tile_rows + col_id * own - HALO
    other = jnp.where(col_id < n_col // 2, row_id - 1, row_id + 1)
    bands = jnp.stack([row_id, other])
    reach = tile_reach[jnp.clip(bands, 0, n_row - 1)]
    bands = bands[:, None]
    tiles = jnp.arange(n_col, dtype=jnp.int32)[None, :]
    row_lo = jnp.maximum(bands * tile_rows - reach[:, :, 0], 0) - first_row
    row_hi = jnp.minimum((bands + 1) * tile_rows + reach[:, :, 1], n_row * tile_rows) - first_row
    row_hi = jnp.where((bands >= 0) & (bands < n_row), row_hi, 0)
    col_lo = jnp.where(tiles > 0, MARGIN - reach[:, :, 2], MARGIN)
    col_hi = jnp.where(tiles < n_col - 1, MARGIN + tile_cols + reach[:, :, 3], MARGIN + tile_cols)
    return jnp.stack([row_lo, row_hi, col_lo, col_hi]).reshape(4, 2 * n_col).astype(jnp.int32)


def halo_rows(rows, n_all):
    own = rows.shape[0]
    above, below = [], []
    left, hop = HALO, 1
    while left > 0:
        take = min(own, left)
        above.insert(0, lax.ppermute(rows[own - take :], ("row", "col"), [(i, i + hop) for i in range(n_all - hop)]))
        below.append(lax.ppermute(rows[:take], ("row", "col"), [(i + hop, i) for i in range(n_all - hop)]))
        left -= take
        hop += 1
    return above, below


def on_device(
    latent, tile_reach, first_weight, first_bias, second_weight, second_bias, proj_weight,
    upper_weight, upper_bias, lower_weight, lower_bias,
):
    chans = first_weight.shape[2]
    dc = proj_weight.shape[1]
    tile_rows = latent.shape[0]
    tile_cols = latent.shape[1] // chans
    n_row = lax.axis_size("row")
    n_col = lax.axis_size("col")
    row_id = lax.axis_index("row")
    col_id = lax.axis_index("col")
    own = tile_rows // n_col
    geom = (n_row, n_col, tile_rows, tile_cols, own)

    moved = lax.all_to_all(
        latent.reshape(n_col, own, tile_cols * chans), "col", split_axis=0, concat_axis=0
    )
    biases = jnp.stack(
        [jnp.pad(b, (0, dc - b.shape[0])) for b in (first_bias, second_bias, upper_bias, lower_bias)]
    )
    ids = jnp.stack([row_id, col_id]).astype(jnp.int32)
    bounds = tile_bounds(tile_reach, row_id, col_id, n_row, n_col, tile_rows, tile_cols, own)
    bounds = jnp.broadcast_to(bounds[:, :, None], bounds.shape + (128,))
    early = (ids, bounds, biases, setup_call(first_weight, second_weight))
    moved, early = lax.optimization_barrier((moved, early))
    ids, bounds, biases, taps = early

    rows = moved.transpose(1, 0, 2)
    above, below = halo_rows(rows, n_row * n_col)
    return main_call(
        geom, ids, above + [rows] + below, bounds, *taps, biases, proj_weight,
        upper_weight.reshape(9, dc, dc), lower_weight.reshape(9, dc, dc), chans,
    )


def solution(mesh):
    in_specs = (P("row", "col"), P(), P(), P(), P(), P(), P(), P(), P(), P(), P())
    out_specs = P(("row", "col"), None, None)
    return jax.shard_map(
        on_device, mesh=mesh, in_specs=in_specs, out_specs=out_specs, check_vma=False
    )
```

```python
import jax
import jax.numpy as jnp
from jax import lax
from jax.experimental import pallas as pl
from jax.experimental.pallas import tpu as pltpu
from jax.sharding import PartitionSpec as P

BF = jnp.bfloat16
F32 = jnp.float32
MARGIN = 4
HALO = 3
VMEM_LIMIT = 62 * 1024 * 1024
PAIR_ORDER = ((0, 0), (0, 1), (1, 0), (1, 1), (0, 2), (1, 2), (2, 0), (2, 1), (2, 2))


def silu(v):
    return v / (1.0 + jnp.exp(-v))


def tap_kernel(w_ref, main_ref, rest_ref):
    chans = w_ref.shape[2]
    main = chans // 128 * 128
    rest = chans - main
    depth = main_ref.shape[0] // 3
    main_ref[...] = jnp.zeros_like(main_ref)
    rest_ref[...] = jnp.zeros_like(rest_ref)
    for dy in range(3):
        for dx in range(3):
            main_ref[dy * depth + dx * main : dy * depth + dx * main + main, :] = w_ref[dy, dx, :main, :main]
            at = 3 * main + dx * rest
            main_ref[dy * depth + at : dy * depth + at + rest, :] = w_ref[dy, dx, main:, :main]
    for dx in range(3):
        for lo, n, at in ((0, main, dx * main), (main, rest, 3 * main + dx * rest)):
            tails = [w_ref[dy, dx, lo : lo + n, main:].astype(F32) for dy in range(3)]
            rest_ref[at : at + n, :128] = jnp.concatenate(tails[:2], axis=1).astype(BF)
            rest_ref[at : at + n, 128 : 128 + rest] = tails[2].astype(BF)


def setup_kernel(w1_ref, w2_ref, m1_ref, r1_ref, m2_ref, r2_ref):
    tap_kernel(w1_ref, m1_ref, r1_ref)
    tap_kernel(w2_ref, m2_ref, r2_ref)


def setup_call(w1, w2):
    chans = w1.shape[2]
    main = chans // 128 * 128
    rest = chans - main
    assert 2 * rest == 128
    depth = 3 * main + 4 * rest
    taps = [jax.ShapeDtypeStruct((3 * depth, main), BF), jax.ShapeDtypeStruct((depth, 256), BF)]
    return pl.pallas_call(
        setup_kernel,
        out_shape=taps + taps,
        compiler_params=pltpu.CompilerParams(vmem_limit_bytes=VMEM_LIMIT),
        cost_estimate=pl.CostEstimate(flops=0, bytes_accessed=8 << 20, transcendentals=0),
    )(w1, w2)


def put_cells(main_ref, rest_ref, r, v, main):
    span = v.shape[0]
    main_ref[r, pl.ds(1, span)] = v[:, :, :main].astype(BF)
    rest = v[:, :, main:]
    none = jnp.zeros((1,) + rest.shape[1:], F32)
    before = jnp.concatenate([none, rest[:-1]], axis=0)
    after = jnp.concatenate([rest[1:], none], axis=0)
    rest_ref[r, :, :, :128] = (before + pltpu.roll(rest, 64, 2)).astype(BF)
    rest_ref[r, :, :, 128:] = after.astype(BF)


def conv_group(main_ref, rest_ref, w_main, w_rest, start, rows, tail):
    span, slots = rest_ref.shape[1:3]
    main = main_ref.shape[3]
    size = rows * span * slots
    parts = []
    for dy in range(3):
        for dx in range(3):
            parts.append(main_ref[pl.ds(start + dy, rows), pl.ds(dx, span)].reshape(size, main))
        parts.append(rest_ref[pl.ds(start + dy, rows)].reshape(size, 256))
    big = jnp.dot(jnp.concatenate(parts, axis=1), w_main[...], preferred_element_type=F32)
    fresh = start + 2 if tail is not None else start
    count = rows + 2 - (fresh - start)
    size = count * span * slots
    parts = [main_ref[pl.ds(fresh, count), pl.ds(dx, span)].reshape(size, main) for dx in range(3)]
    parts.append(rest_ref[pl.ds(fresh, count)].reshape(size, 256))
    part = jnp.dot(jnp.concatenate(parts, axis=1), w_rest[...], preferred_element_type=F32)
    part = part.reshape(count, span, slots, 256)
    if tail is not None:
        part = jnp.concatenate([tail, part], axis=0)
    rest = part[:-2, :, :, :128] + pltpu.roll(part[1:-1, :, :, :128], 64, 3) + part[2:, :, :, 128:]
    return big.reshape(rows, span, slots, main), rest, part[-2:]


def tile_body(geom, chans, tall, params, m1, r1, b1_ref, m2, r2, b2_ref, canvas, xm, xr, am, ar, cells_ref, waits):
    n_row, n_col, tile_rows, tile_cols, own = geom
    slots = 2 * n_col
    span = tile_cols + 2 * MARGIN
    main = chans // 128 * 128
    lanes = main + 128
    rows_x = own + 2 * HALO
    width = n_col * tile_cols
    live = (lax.broadcasted_iota(jnp.int32, (1, 1, 128), 2) < chans - main).astype(F32)
    cell = lax.broadcasted_iota(jnp.int32, (span, slots, 128), 0)
    slot = lax.broadcasted_iota(jnp.int32, (slots, 128), 0)

    def per_slot(k):
        out = jnp.zeros((slots, 128), jnp.int32)
        for i in range(slots):
            out = jnp.where(slot == i, params[k * slots + i], out)
        return out

    bounds_ref = [per_slot(k) for k in range(4)]
    cols_ok = ((cell >= bounds_ref[2]) & (cell < bounds_ref[3])).astype(F32)
    xm[...] = jnp.zeros_like(xm)
    am[...] = jnp.zeros_like(am)

    def mask_of(r):
        row = jnp.zeros((slots, 128), jnp.int32) + r
        rows_ok = ((row >= bounds_ref[0]) & (row < bounds_ref[1])).astype(F32)
        return cols_ok * rows_ok

    def wide(m):
        return jnp.concatenate([m] * (lanes // 128), axis=2)

    r = 0
    for piece in tall:
        for k in range(piece.shape[0]):
            cols = []
            for c in range(tile_cols):
                lo = c * chans
                off = lo % 128
                v = piece[k, :, lo - off : lo - off + lanes].astype(F32)
                if off:
                    v = pltpu.roll(v, lanes - off, 1)
                cols.append(v)
            cells_ref[...] = jnp.stack(cols, axis=0)
            v = cells_ref[...]
            v = jnp.concatenate([v[:, :, :main], v[:, :, main:] * live], axis=2)
            v = jnp.concatenate(
                [pltpu.roll(v[-MARGIN:], 1, 1), v, pltpu.roll(v[:MARGIN], n_col - 1, 1)], axis=0)
            v = jnp.concatenate([v, v], axis=1)
            put_cells(xm, xr, r, v * wide(mask_of(r)), main)
            r += 1

    group1 = (rows_x - 2) // 2
    def first(g, carry):
        big, rest, tail = conv_group(xm, xr, m1, r1, g * group1, group1, carry)
        for i in range(group1):
            a = g * group1 + i
            v = jnp.concatenate([big[i], rest[i] * live], axis=2) + b1_ref[...]
            put_cells(am, ar, a, silu(v) * wide(mask_of(a + 1)), main)
        return tail
    waits[0]()
    tail = None
    for g in range(2):
        tail = first(g, tail)

    group2 = (rows_x - 4) // 2
    def second(g, carry):
        big, rest, tail = conv_group(am, ar, m2, r2, g * group2, group2, carry)
        for i in range(group2):
            a = g * group2 + i
            v = jnp.concatenate([big[i], rest[i] * live], axis=2) + b2_ref[...]
            x_rest = pltpu.roll(xr[a + 2, :, :, :128].astype(F32), 64, 2) * live
            x = jnp.concatenate([xm[a + 2, pl.ds(1, span)].astype(F32), x_rest], axis=2)
            mask = mask_of(a + 2)
            y = ((v + x) * wide(mask)).astype(BF).astype(F32)

            def fold(u):
                u = u[:, :n_col] + u[:, n_col:]
                mid = u[MARGIN:-MARGIN]
                return jnp.concatenate(
                    [
                        mid[:MARGIN] + pltpu.roll(u[-MARGIN:], 1, 1),
                        mid[MARGIN:-MARGIN],
                        mid[-MARGIN:] + pltpu.roll(u[:MARGIN], n_col - 1, 1),
                    ],
                    axis=0,
                )

            count = fold(mask)
            blend = fold(y) * wide(jnp.where(count > 0, 1.0 / jnp.maximum(count, 1.0), 0.0))
            for c in range(tile_cols):
                for lane in range(lanes // 128):
                    canvas[lane, pl.ds(a * width + c, n_col, stride=tile_cols), :] = blend[c, :, lane * 128 : lane * 128 + 128]
        return tail
    waits[1]()
    tail = None
    for g in range(2):
        tail = second(g, tail)


def tile_scratch(geom, chans):
    n_row, n_col, tile_rows, tile_cols, own = geom
    slots = 2 * n_col
    span = tile_cols + 2 * MARGIN
    main = chans // 128 * 128
    rows_x = own + 2 * HALO
    return [
        pltpu.VMEM((main // 128 + 1, (own + 2) * n_col * tile_cols, 128), F32),
        pltpu.VMEM((rows_x, span + 2, slots, main), BF),
        pltpu.VMEM((rows_x, span, slots, 256), BF),
        pltpu.VMEM((rows_x - 2, span + 2, slots, main), BF),
        pltpu.VMEM((rows_x - 2, span, slots, 256), BF),
        pltpu.VMEM((tile_cols, n_col, main + 128), F32),
    ]


def halves(first, second, third):
    half = 0.5 * second
    return first + half, third + half, half


def weight_kernel(upper_ref, lower_ref, upper_out, pair_out):
    w = [[upper_ref[3 * dy + dx].astype(F32) for dx in range(3)] for dy in range(3)]
    rows = [halves(w[0][dx], w[1][dx], w[2][dx]) for dx in range(3)]
    both = [halves(rows[0][r], rows[1][r], rows[2][r]) for r in range(3)]
    for i, (r, c) in enumerate(PAIR_ORDER):
        upper_out[i] = both[r][c].astype(BF)
    for dy in range(3):
        ends = 0.5 * (lower_ref[3 * dy].astype(F32) + lower_ref[3 * dy + 2].astype(F32))
        mid = 0.5 * lower_ref[3 * dy + 1].astype(F32)
        pair_out[0, dy] = (ends + mid).astype(BF)
        pair_out[1, dy] = (ends - mid).astype(BF)


def weight_call(upper, lower):
    dc = upper.shape[2]
    step = 128
    return pl.pallas_call(
        weight_kernel,
        grid=(dc // step,),
        out_shape=(jax.ShapeDtypeStruct((9, dc, dc), BF), jax.ShapeDtypeStruct((2, 3, dc, dc), BF)),
        in_specs=[pl.BlockSpec((9, step, dc), lambda i: (0, i, 0))] * 2,
        out_specs=(
            pl.BlockSpec((9, step, dc), lambda i: (0, i, 0)),
            pl.BlockSpec((2, 3, step, dc), lambda i: (0, 0, i, 0)),
        ),
        compiler_params=pltpu.CompilerParams(vmem_limit_bytes=VMEM_LIMIT),
        cost_estimate=pl.CostEstimate(flops=40 * dc * dc, bytes_accessed=66 * dc * dc, transcendentals=0),
    )(upper, lower)


def decoder_body(
    keep, canvas, proj_ref, ub_ref, lb_ref, out_hbm, out_ref, out_sems, hid, beyond, across, down, down_beyond,
    down_across, first, comps, edge, zipped, upper_v, lower_v, waits,
):
    rows, width, dc = hid.shape
    steps = rows - 1
    own = rows - 2
    chans = proj_ref.shape[0]
    main = chans // 128 * 128

    edge[...] = jnp.zeros_like(edge)
    first[...] = jnp.zeros_like(first)
    waits[0]()
    last = None
    for r in range(rows):
        at = pl.ds(r * width, width)
        x = jnp.concatenate([canvas[lane, at, :] for lane in range(main // 128)], axis=1).astype(BF)
        rest = canvas[main // 128, at, :].astype(BF)[:, : chans - main]
        h = jnp.dot(x, proj_ref[:main, :], preferred_element_type=F32)
        h = h + jnp.dot(rest, proj_ref[main:, :], preferred_element_type=F32)
        h = h.astype(BF)
        hid[r] = h
        h = h.astype(F32)
        edge[0, pl.ds(8, width), :] = h
        first[pl.ds(r, 1), :] = h[:1]
        b = edge[0, pl.ds(9, width), :]
        beyond[r] = b.astype(BF)
        across[r] = (h - b).astype(BF)
        if last is not None:
            down[r - 1] = (last[0] - h).astype(BF)
            down_beyond[r - 1] = (last[1] - b).astype(BF)
            down_across[r - 1] = ((last[0] - h) - (last[1] - b)).astype(BF)
        last = (h, b)

    waits[1]()
    near, far = first[pl.ds(0, 16), :], first[pl.ds(1, 16), :]
    none = jnp.zeros((16, dc), BF)

    def side(ref, start, extra):
        return jnp.concatenate([ref[pl.ds(start, steps)].reshape(steps * width, dc), extra.astype(BF)], axis=0)

    def product(parts, at):
        rhs = upper_v[pl.ds(at, len(parts))].reshape(len(parts) * dc, dc)
        return jnp.dot(jnp.concatenate(parts, axis=1), rhs, preferred_element_type=F32)

    sums = product([side(hid, 0, none), side(beyond, 0, near), side(hid, 1, none), side(beyond, 1, far)], 0)
    cols = product([side(across, 0, -near), side(across, 1, -far)], 4)
    lines = product([side(down, 0, none), side(down_beyond, 0, near - far)], 6)
    cross = product([side(down_across, 0, far - near)], 8)
    col_id = lax.broadcasted_iota(jnp.int32, (width, 1), 0)
    for p in (1, 0):
        if p == 1:
            straight, turned = sums + lines, cols + cross
        else:
            straight, turned = sums - lines, cols - cross
        odd = silu(straight + turned + ub_ref[...])
        even = silu(straight - turned + ub_ref[...])
        for k in range(steps):
            scale = 1.0
            if k == 0 and p == 1:
                scale = keep[0]
            if k == steps - 1 and p == 0:
                scale = keep[1]
            o = (odd[k * width : (k + 1) * width] * scale).astype(BF).astype(F32)
            after = (even[k * width : (k + 1) * width] * scale).astype(BF).astype(F32)
            after = jnp.where(col_id < width - 1, after, 0.0)
            start = (even[steps * width + k : steps * width + k + 1] * scale).astype(BF).astype(F32)
            edge[0, pl.ds(8, width), :] = o
            edge[1, pl.ds(8, width), :] = after
            edge[1, pl.ds(7, 1), :] = start
            e = edge[1, pl.ds(7, width), :]
            at = 2 * k + 1 - p
            comps[0, at] = (edge[0, pl.ds(7, width), :] - o).astype(BF)
            comps[1, at] = (e + o).astype(BF)
            comps[2, at] = (o - e).astype(BF)
            comps[3, at] = (e - after).astype(BF)

    waits[2]()
    group = own
    copies = []
    for n in range(2 * own // group):
        start = n * group
        prods = []
        for i in range(4):
            lhs = jnp.concatenate(
                [comps[i, pl.ds(start + dy, group)].reshape(group * width, dc) for dy in range(3)], axis=1)
            prods.append(jnp.dot(lhs, lower_v[i].reshape(3 * dc, dc), preferred_element_type=F32))
        both = (prods[0] + (prods[1] + prods[2]), (prods[1] - prods[2]) - prods[3])
        for g in range(group):
            base = hid[1 + (start + g) // 2].astype(F32) + lb_ref[...]
            for q in range(2):
                v = both[q][g * width : (g + 1) * width] + base
                for lane in range(dc // 128):
                    zipped[lane, pl.ds(g * 2 * width + q, width, stride=2), :] = v[:, lane * 128 : lane * 128 + 128]
            for lane in range(dc // 128):
                out_ref[start + g, :, pl.ds(lane * 128, 128)] = zipped[lane, pl.ds(g * 2 * width, 2 * width), :].astype(BF)
        copy = pltpu.make_async_copy(out_ref.at[pl.ds(start, group)], out_hbm.at[pl.ds(start, group)], out_sems.at[n])
        copy.start()
        copies.append(copy)
    for copy in copies:
        copy.wait()


def main_kernel(geom, chans, n_tall, params, bias_ref, *refs):
    n_row, n_col, tile_rows, tile_cols, own = geom
    m1_in, r1_in, m2_in, r2_in, proj_in, upper_in, pair_in, lower_in = refs[:8]
    tall, refs = refs[8 : 8 + n_tall], refs[8 + n_tall :]
    (out_hbm, canvas, xm, xr, am, ar, cells_ref, hid, beyond, across, down, down_beyond, down_across, first, comps,
     edge, zipped, out_ref, m1, r1, m2, r2, proj, upper, lower, sems, out_sems) = refs
    moves = [
        (m1_in, m1), (r1_in, r1), (m2_in, m2), (r2_in, r2), (proj_in, proj), (upper_in, upper),
        (pair_in, lower.at[pl.ds(1, 2)]), (lower_in.at[:, 0], lower.at[0]), (lower_in.at[:, 2], lower.at[3]),
    ]
    copies = [pltpu.make_async_copy(src, dst, sems.at[i]) for i, (src, dst) in enumerate(moves)]
    for copy in copies:
        copy.start()

    def wait_for(*which):
        def wait():
            for i in which:
                copies[i].wait()
        return wait

    base = 8 * n_col
    first_row = params[base] * tile_rows + params[base + 1] * own
    keep = (
        jnp.where(first_row > 0, 1.0, 0.0),
        jnp.where(first_row + own < n_row * tile_rows, 1.0, 0.0),
    )
    lanes = chans // 128 * 128 + 128
    bias1, bias2 = bias_ref.at[pl.ds(0, 1), pl.ds(0, lanes)], bias_ref.at[pl.ds(1, 1), pl.ds(0, lanes)]
    tile_body(
        geom, chans, tall, params, m1, r1, bias1, m2, r2, bias2, canvas, xm, xr, am, ar, cells_ref,
        (wait_for(0, 1), wait_for(2, 3)),
    )
    decoder_body(
        keep, canvas, proj, bias_ref.at[pl.ds(2, 1)], bias_ref.at[pl.ds(3, 1)], out_hbm, out_ref, out_sems,
        hid, beyond, across, down, down_beyond, down_across, first, comps, edge, zipped, upper, lower,
        (wait_for(4), wait_for(5), wait_for(6, 7, 8)),
    )


def main_call(geom, params, tall, m1, r1, m2, r2, biases, proj, upper, pair, lower, chans):
    n_row, n_col, tile_rows, tile_cols, own = geom
    width = n_col * tile_cols
    rows = own + 2
    dc = proj.shape[1]
    vm = pl.BlockSpec(memory_space=pltpu.VMEM)
    anyspace = pl.BlockSpec(memory_space=pl.ANY)

    def kernel(*refs):
        main_kernel(geom, chans, len(tall), *refs)

    return pl.pallas_call(
        kernel,
        out_shape=jax.ShapeDtypeStruct((2 * own, 2 * width, dc), BF),
        in_specs=[pl.BlockSpec(memory_space=pltpu.SMEM), vm] + [anyspace] * 8 + [vm] * len(tall),
        out_specs=anyspace,
        scratch_shapes=tile_scratch(geom, chans)
        + [pltpu.VMEM((rows, width, dc), BF)] * 3
        + [pltpu.VMEM((rows - 1, width, dc), BF)] * 3
        + [
            pltpu.VMEM((24, dc), F32),
            pltpu.VMEM((4, 2 * own + 2, width, dc), BF),
            pltpu.VMEM((2, width + 16, dc), F32),
            pltpu.VMEM((dc // 128, 2 * own * width, 128), F32),
            pltpu.VMEM((2 * own, 2 * width, dc), BF),
        ]
        + [pltpu.VMEM(u.shape, BF) for u in (m1, r1, m2, r2, proj, upper)]
        + [
            pltpu.VMEM((4, 3, dc, dc), BF),
            pltpu.SemaphoreType.DMA((9,)),
            pltpu.SemaphoreType.DMA((2,)),
        ],
        compiler_params=pltpu.CompilerParams(vmem_limit_bytes=VMEM_LIMIT),
        cost_estimate=pl.CostEstimate(flops=25_000_000_000, bytes_accessed=20 << 20, transcendentals=0),
    )(params, biases, m1, r1, m2, r2, proj, upper, pair, lower, *tall)


def tile_bounds(tile_reach, row_id, col_id, n_row, n_col, tile_rows, tile_cols, own):
    first_row = row_id * tile_rows + col_id * own - HALO
    other = jnp.where(col_id < n_col // 2, row_id - 1, row_id + 1)
    bands = jnp.stack([row_id, other])
    reach = tile_reach[jnp.clip(bands, 0, n_row - 1)]
    bands = bands[:, None]
    tiles = jnp.arange(n_col, dtype=jnp.int32)[None, :]
    row_lo = jnp.maximum(bands * tile_rows - reach[:, :, 0], 0) - first_row
    row_hi = jnp.minimum((bands + 1) * tile_rows + reach[:, :, 1], n_row * tile_rows) - first_row
    row_hi = jnp.where((bands >= 0) & (bands < n_row), row_hi, 0)
    col_lo = jnp.where(tiles > 0, MARGIN - reach[:, :, 2], MARGIN)
    col_hi = jnp.where(tiles < n_col - 1, MARGIN + tile_cols + reach[:, :, 3], MARGIN + tile_cols)
    return jnp.stack([row_lo, row_hi, col_lo, col_hi]).reshape(4, 2 * n_col).astype(jnp.int32)


def halo_rows(rows, n_all):
    own = rows.shape[0]
    above, below = [], []
    left, hop = HALO, 1
    while left > 0:
        take = min(own, left)
        above.insert(0, lax.ppermute(rows[own - take :], ("row", "col"), [(i, i + hop) for i in range(n_all - hop)]))
        below.append(lax.ppermute(rows[:take], ("row", "col"), [(i + hop, i) for i in range(n_all - hop)]))
        left -= take
        hop += 1
    return above, below


def on_device(
    latent, tile_reach, first_weight, first_bias, second_weight, second_bias, proj_weight,
    upper_weight, upper_bias, lower_weight, lower_bias,
):
    chans = first_weight.shape[2]
    dc = proj_weight.shape[1]
    tile_rows = latent.shape[0]
    tile_cols = latent.shape[1] // chans
    n_row = lax.axis_size("row")
    n_col = lax.axis_size("col")
    row_id = lax.axis_index("row")
    col_id = lax.axis_index("col")
    own = tile_rows // n_col
    geom = (n_row, n_col, tile_rows, tile_cols, own)

    moved = lax.all_to_all(
        latent.reshape(n_col, own, tile_cols * chans), "col", split_axis=0, concat_axis=0
    )
    biases = jnp.stack(
        [jnp.pad(b, (0, dc - b.shape[0])) for b in (first_bias, second_bias, upper_bias, lower_bias)]
    )
    bounds = tile_bounds(tile_reach, row_id, col_id, n_row, n_col, tile_rows, tile_cols, own)
    params = jnp.concatenate([bounds.reshape(-1), jnp.stack([row_id, col_id]).astype(jnp.int32)])
    early = (params, biases, setup_call(first_weight, second_weight))
    moved, early, upper_weight, lower_weight = lax.optimization_barrier(
        (moved, early, upper_weight, lower_weight)
    )
    params, biases, taps = early

    rows = moved.transpose(1, 0, 2)
    above, below = halo_rows(rows, n_row * n_col)
    upper, pair = weight_call(upper_weight.reshape(9, dc, dc), lower_weight.reshape(9, dc, dc))
    return main_call(
        geom, params, above + [rows] + below, *taps, biases, proj_weight, upper, pair, lower_weight, chans,
    )


def solution(mesh):
    in_specs = (P("row", "col"), P(), P(), P(), P(), P(), P(), P(), P(), P(), P())
    out_specs = P(("row", "col"), None, None)
    return jax.shard_map(
        on_device, mesh=mesh, in_specs=in_specs, out_specs=out_specs, check_vma=False
    )
```

```python
import jax
import jax.numpy as jnp
from jax import lax
from jax.experimental import pallas as pl
from jax.experimental.pallas import tpu as pltpu
from jax.sharding import PartitionSpec as P

BF = jnp.bfloat16
F32 = jnp.float32
MARGIN = 4
HALO = 3
VMEM_LIMIT = 62 * 1024 * 1024
PAIR_ORDER = ((0, 0), (0, 1), (1, 0), (1, 1), (0, 2), (1, 2), (2, 0), (2, 1), (2, 2))


def silu(v):
    return v / (1.0 + jnp.exp(-v))


def tap_kernel(w_ref, main_ref, rest_ref):
    chans = w_ref.shape[2]
    main = chans // 128 * 128
    rest = chans - main
    depth = main_ref.shape[0] // 3
    main_ref[...] = jnp.zeros_like(main_ref)
    rest_ref[...] = jnp.zeros_like(rest_ref)
    for dy in range(3):
        for dx in range(3):
            main_ref[dy * depth + dx * main : dy * depth + dx * main + main, :] = w_ref[dy, dx, :main, :main]
            at = 3 * main + dx * rest
            main_ref[dy * depth + at : dy * depth + at + rest, :] = w_ref[dy, dx, main:, :main]
    for dx in range(3):
        for lo, n, at in ((0, main, dx * main), (main, rest, 3 * main + dx * rest)):
            tails = [w_ref[dy, dx, lo : lo + n, main:].astype(F32) for dy in range(3)]
            rest_ref[at : at + n, :128] = jnp.concatenate(tails[:2], axis=1).astype(BF)
            rest_ref[at : at + n, 128 : 128 + rest] = tails[2].astype(BF)


def setup_kernel(w1_ref, w2_ref, m1_ref, r1_ref, m2_ref, r2_ref):
    tap_kernel(w1_ref, m1_ref, r1_ref)
    tap_kernel(w2_ref, m2_ref, r2_ref)


def setup_call(w1, w2):
    chans = w1.shape[2]
    main = chans // 128 * 128
    rest = chans - main
    assert 2 * rest == 128
    depth = 3 * main + 4 * rest
    taps = [jax.ShapeDtypeStruct((3 * depth, main), BF), jax.ShapeDtypeStruct((depth, 256), BF)]
    return pl.pallas_call(
        setup_kernel,
        out_shape=taps + taps,
        compiler_params=pltpu.CompilerParams(vmem_limit_bytes=VMEM_LIMIT),
        cost_estimate=pl.CostEstimate(flops=0, bytes_accessed=8 << 20, transcendentals=0),
    )(w1, w2)


def put_cells(main_ref, rest_ref, r, v, main):
    span = v.shape[0]
    main_ref[r, pl.ds(1, span)] = v[:, :, :main].astype(BF)
    rest = v[:, :, main:]
    none = jnp.zeros((1,) + rest.shape[1:], F32)
    before = jnp.concatenate([none, rest[:-1]], axis=0)
    after = jnp.concatenate([rest[1:], none], axis=0)
    rest_ref[r, :, :, :128] = (before + pltpu.roll(rest, 64, 2)).astype(BF)
    rest_ref[r, :, :, 128:] = after.astype(BF)


def conv_group(main_ref, rest_ref, w_main, w_rest, start, rows, tail):
    span, slots = rest_ref.shape[1:3]
    main = main_ref.shape[3]
    size = rows * span * slots
    parts = []
    for dy in range(3):
        for dx in range(3):
            parts.append(main_ref[pl.ds(start + dy, rows), pl.ds(dx, span)].reshape(size, main))
        parts.append(rest_ref[pl.ds(start + dy, rows)].reshape(size, 256))
    big = jnp.dot(jnp.concatenate(parts, axis=1), w_main[...], preferred_element_type=F32)
    fresh = start + 2 if tail is not None else start
    count = rows + 2 - (fresh - start)
    size = count * span * slots
    parts = [main_ref[pl.ds(fresh, count), pl.ds(dx, span)].reshape(size, main) for dx in range(3)]
    parts.append(rest_ref[pl.ds(fresh, count)].reshape(size, 256))
    part = jnp.dot(jnp.concatenate(parts, axis=1), w_rest[...], preferred_element_type=F32)
    part = part.reshape(count, span, slots, 256)
    if tail is not None:
        part = jnp.concatenate([tail, part], axis=0)
    rest = part[:-2, :, :, :128] + pltpu.roll(part[1:-1, :, :, :128], 64, 3) + part[2:, :, :, 128:]
    return big.reshape(rows, span, slots, main), rest, part[-2:]


def tile_body(geom, chans, tall, params, m1, r1, b1_ref, m2, r2, b2_ref, canvas, xm, xr, am, ar, cells_ref, waits):
    n_row, n_col, tile_rows, tile_cols, own = geom
    slots = 2 * n_col
    span = tile_cols + 2 * MARGIN
    main = chans // 128 * 128
    lanes = main + 128
    rows_x = own + 2 * HALO
    width = n_col * tile_cols
    live = (lax.broadcasted_iota(jnp.int32, (1, 1, 128), 2) < chans - main).astype(F32)
    cell = lax.broadcasted_iota(jnp.int32, (span, slots, 128), 0)
    slot = lax.broadcasted_iota(jnp.int32, (slots, 128), 0)

    def per_slot(k):
        out = jnp.zeros((slots, 128), jnp.int32)
        for i in range(slots):
            out = jnp.where(slot == i, params[k * slots + i], out)
        return out

    bounds_ref = [per_slot(k) for k in range(4)]
    cols_ok = ((cell >= bounds_ref[2]) & (cell < bounds_ref[3])).astype(F32)
    xm[...] = jnp.zeros_like(xm)
    am[...] = jnp.zeros_like(am)

    def mask_of(r):
        row = jnp.zeros((slots, 128), jnp.int32) + r
        rows_ok = ((row >= bounds_ref[0]) & (row < bounds_ref[1])).astype(F32)
        return cols_ok * rows_ok

    def wide(m):
        return jnp.concatenate([m] * (lanes // 128), axis=2)

    r = 0
    is_odd = lax.rem(params[4 * slots + 1], 2) == 1
    for on_odd, on_even in tall:
        for k in range(on_odd.shape[0]):
            cols = []
            for c in range(tile_cols):
                lo = c * chans
                off = lo % 128
                at = slice(lo - off, lo - off + lanes)
                v = on_odd[k, :, at].astype(F32)
                if on_even is not on_odd:
                    v = jnp.where(is_odd, v, on_even[k, :, at].astype(F32))
                if off:
                    v = pltpu.roll(v, lanes - off, 1)
                cols.append(v)
            cells_ref[...] = jnp.stack(cols, axis=0)
            v = cells_ref[...]
            v = jnp.concatenate([v[:, :, :main], v[:, :, main:] * live], axis=2)
            v = jnp.concatenate(
                [pltpu.roll(v[-MARGIN:], 1, 1), v, pltpu.roll(v[:MARGIN], n_col - 1, 1)], axis=0)
            v = jnp.concatenate([v, v], axis=1)
            put_cells(xm, xr, r, v * wide(mask_of(r)), main)
            r += 1

    group1 = (rows_x - 2) // 2
    def first(g, carry):
        big, rest, tail = conv_group(xm, xr, m1, r1, g * group1, group1, carry)
        for i in range(group1):
            a = g * group1 + i
            v = jnp.concatenate([big[i], rest[i] * live], axis=2) + b1_ref[...]
            put_cells(am, ar, a, silu(v) * wide(mask_of(a + 1)), main)
        return tail
    waits[0]()
    tail = None
    for g in range(2):
        tail = first(g, tail)

    group2 = (rows_x - 4) // 2
    def second(g, carry):
        waits[2](g)
        big, rest, tail = conv_group(am, ar, m2, r2, g * group2, group2, carry)
        for i in range(group2):
            a = g * group2 + i
            v = jnp.concatenate([big[i], rest[i] * live], axis=2) + b2_ref[...]
            x_rest = pltpu.roll(xr[a + 2, :, :, :128].astype(F32), 64, 2) * live
            x = jnp.concatenate([xm[a + 2, pl.ds(1, span)].astype(F32), x_rest], axis=2)
            mask = mask_of(a + 2)
            y = ((v + x) * wide(mask)).astype(BF).astype(F32)

            def fold(u):
                u = u[:, :n_col] + u[:, n_col:]
                mid = u[MARGIN:-MARGIN]
                return jnp.concatenate(
                    [
                        mid[:MARGIN] + pltpu.roll(u[-MARGIN:], 1, 1),
                        mid[MARGIN:-MARGIN],
                        mid[-MARGIN:] + pltpu.roll(u[:MARGIN], n_col - 1, 1),
                    ],
                    axis=0,
                )

            count = fold(mask)
            blend = fold(y) * wide(jnp.where(count > 0, 1.0 / jnp.maximum(count, 1.0), 0.0))
            for c in range(tile_cols):
                for lane in range(lanes // 128):
                    canvas[lane, pl.ds(a * width + c, n_col, stride=tile_cols), :] = blend[c, :, lane * 128 : lane * 128 + 128]
        return tail
    waits[1]()
    tail = None
    for g in range(2):
        tail = second(g, tail)


def tile_scratch(geom, chans):
    n_row, n_col, tile_rows, tile_cols, own = geom
    slots = 2 * n_col
    span = tile_cols + 2 * MARGIN
    main = chans // 128 * 128
    rows_x = own + 2 * HALO
    return [
        pltpu.VMEM((main // 128 + 1, (own + 2) * n_col * tile_cols, 128), F32),
        pltpu.VMEM((rows_x, span + 2, slots, main), BF),
        pltpu.VMEM((rows_x, span, slots, 256), BF),
        pltpu.VMEM((rows_x - 2, span + 2, slots, main), BF),
        pltpu.VMEM((rows_x - 2, span, slots, 256), BF),
        pltpu.VMEM((tile_cols, n_col, main + 128), F32),
    ]


def halves(first, second, third):
    half = 0.5 * second
    return first + half, third + half, half


def upper_kernel(w_hbm, out_hbm, w_ref, out_ref, in_sems, out_sems):
    step = w_ref.shape[1] // 4
    parts = [pl.ds(i * step, step) for i in range(4)]
    reads = [pltpu.make_async_copy(w_hbm.at[:, at], w_ref.at[:, at], in_sems.at[i]) for i, at in enumerate(parts)]
    writes = [pltpu.make_async_copy(out_ref.at[:, at], out_hbm.at[:, at], out_sems.at[i]) for i, at in enumerate(parts)]
    for read in reads:
        read.start()
    for read, write, at in zip(reads, writes, parts):
        read.wait()
        w = [[w_ref[3 * dy + dx, at, :].astype(F32) for dx in range(3)] for dy in range(3)]
        rows = [halves(w[0][dx], w[1][dx], w[2][dx]) for dx in range(3)]
        both = [halves(rows[0][r], rows[1][r], rows[2][r]) for r in range(3)]
        for i, (r, c) in enumerate(PAIR_ORDER):
            out_ref[i, at, :] = both[r][c].astype(BF)
        write.start()
    for write in writes:
        write.wait()


def upper_call(w):
    anyspace = pl.BlockSpec(memory_space=pl.ANY)
    return pl.pallas_call(
        upper_kernel,
        out_shape=jax.ShapeDtypeStruct(w.shape, BF),
        in_specs=[anyspace],
        out_specs=anyspace,
        scratch_shapes=[pltpu.VMEM(w.shape, BF)] * 2 + [pltpu.SemaphoreType.DMA((4,))] * 2,
        compiler_params=pltpu.CompilerParams(vmem_limit_bytes=VMEM_LIMIT),
        cost_estimate=pl.CostEstimate(flops=0, bytes_accessed=4 * w.size, transcendentals=0),
    )(w)


def pair_part(w, k0, kn):
    ks = pl.ds(k0, kn)
    for dy in range(3):
        ends = 0.5 * (w[0, dy, ks, :].astype(F32) + w[3, dy, ks, :].astype(F32))
        mid = 0.5 * w[1, dy, ks, :].astype(F32)
        w[1, dy, ks, :] = (ends + mid).astype(BF)
        w[2, dy, ks, :] = (ends - mid).astype(BF)


def decoder_body(
    keep, canvas, proj_ref, ub_ref, lb_ref, out_hbm, out_ref, out_sems, hid, beyond, across, down, down_beyond,
    down_across, first, comps, edge, zipped, upper_v, lower_v, waits,
):
    rows, width, dc = hid.shape
    steps = rows - 1
    own = rows - 2
    chans = proj_ref.shape[0]
    main = chans // 128 * 128

    edge[...] = jnp.zeros_like(edge)
    first[...] = jnp.zeros_like(first)
    waits[0]()
    last = None
    for r in range(rows):
        at = pl.ds(r * width, width)
        x = jnp.concatenate([canvas[lane, at, :] for lane in range(main // 128)], axis=1).astype(BF)
        rest = canvas[main // 128, at, :].astype(BF)[:, : chans - main]
        h = jnp.dot(x, proj_ref[:main, :], preferred_element_type=F32)
        h = h + jnp.dot(rest, proj_ref[main:, :], preferred_element_type=F32)
        h = h.astype(BF)
        hid[r] = h
        h = h.astype(F32)
        edge[0, pl.ds(8, width), :] = h
        first[pl.ds(r, 1), :] = h[:1]
        b = edge[0, pl.ds(9, width), :]
        beyond[r] = b.astype(BF)
        across[r] = (h - b).astype(BF)
        if last is not None:
            down[r - 1] = (last[0] - h).astype(BF)
            down_beyond[r - 1] = (last[1] - b).astype(BF)
            down_across[r - 1] = ((last[0] - h) - (last[1] - b)).astype(BF)
        last = (h, b)

    waits[1]()
    near, far = first[pl.ds(0, 16), :], first[pl.ds(1, 16), :]
    none = jnp.zeros((16, dc), BF)

    def side(ref, start, extra):
        return jnp.concatenate([ref[pl.ds(start, steps)].reshape(steps * width, dc), extra.astype(BF)], axis=0)

    def product(parts, at):
        rhs = upper_v[pl.ds(at, len(parts))].reshape(len(parts) * dc, dc)
        return jnp.dot(jnp.concatenate(parts, axis=1), rhs, preferred_element_type=F32)

    sums = product([side(hid, 0, none), side(beyond, 0, near), side(hid, 1, none), side(beyond, 1, far)], 0)
    cols = product([side(across, 0, -near), side(across, 1, -far)], 4)
    lines = product([side(down, 0, none), side(down_beyond, 0, near - far)], 6)
    cross = product([side(down_across, 0, far - near)], 8)
    col_id = lax.broadcasted_iota(jnp.int32, (width, 1), 0)
    for p in (1, 0):
        if p == 1:
            straight, turned = sums + lines, cols + cross
        else:
            straight, turned = sums - lines, cols - cross
        odd = silu(straight + turned + ub_ref[...])
        even = silu(straight - turned + ub_ref[...])
        for k in range(steps):
            scale = 1.0
            if k == 0 and p == 1:
                scale = keep[0]
            if k == steps - 1 and p == 0:
                scale = keep[1]
            o = (odd[k * width : (k + 1) * width] * scale).astype(BF).astype(F32)
            after = (even[k * width : (k + 1) * width] * scale).astype(BF).astype(F32)
            after = jnp.where(col_id < width - 1, after, 0.0)
            start = (even[steps * width + k : steps * width + k + 1] * scale).astype(BF).astype(F32)
            edge[0, pl.ds(8, width), :] = o
            edge[1, pl.ds(8, width), :] = after
            edge[1, pl.ds(7, 1), :] = start
            e = edge[1, pl.ds(7, width), :]
            at = 2 * k + 1 - p
            comps[0, at] = (edge[0, pl.ds(7, width), :] - o).astype(BF)
            comps[1, at] = (e + o).astype(BF)
            comps[2, at] = (o - e).astype(BF)
            comps[3, at] = (e - after).astype(BF)

    group = own
    copies = []
    for n in range(2 * own // group):
        start = n * group
        prods = []
        for i in range(4):
            lhs = jnp.concatenate(
                [comps[i, pl.ds(start + dy, group)].reshape(group * width, dc) for dy in range(3)], axis=1)
            prods.append(jnp.dot(lhs, lower_v[i].reshape(3 * dc, dc), preferred_element_type=F32))
        both = (prods[0] + (prods[1] + prods[2]), (prods[1] - prods[2]) - prods[3])
        for g in range(group):
            base = hid[1 + (start + g) // 2].astype(F32) + lb_ref[...]
            for q in range(2):
                v = both[q][g * width : (g + 1) * width] + base
                for lane in range(dc // 128):
                    zipped[lane, pl.ds(g * 2 * width + q, width, stride=2), :] = v[:, lane * 128 : lane * 128 + 128]
            for lane in range(dc // 128):
                out_ref[start + g, :, pl.ds(lane * 128, 128)] = zipped[lane, pl.ds(g * 2 * width, 2 * width), :].astype(BF)
        copy = pltpu.make_async_copy(out_ref.at[pl.ds(start, group)], out_hbm.at[pl.ds(start, group)], out_sems.at[n])
        copy.start()
        copies.append(copy)
    for copy in copies:
        copy.wait()


def main_kernel(geom, chans, pick, params, bias_ref, *refs):
    n_row, n_col, tile_rows, tile_cols, own = geom
    m1_in, r1_in, m2_in, r2_in, proj_in, upper_in, lower_in = refs[:7]
    n_tall = 1 + max(max(p) for p in pick)
    tall = [(refs[7 + a], refs[7 + b]) for a, b in pick]
    refs = refs[7 + n_tall :]
    (out_hbm, canvas, xm, xr, am, ar, cells_ref, hid, beyond, across, down, down_beyond, down_across, first, comps,
     edge, zipped, out_ref, m1, r1, m2, r2, proj, upper, lower, sems, out_sems) = refs
    moves = [
        (m1_in, m1), (r1_in, r1), (m2_in, m2), (r2_in, r2), (proj_in, proj), (upper_in, upper),
        (lower_in.at[:, 0], lower.at[0]), (lower_in.at[:, 1], lower.at[1]), (lower_in.at[:, 2], lower.at[3]),
    ]
    copies = [pltpu.make_async_copy(src, dst, sems.at[i]) for i, (src, dst) in enumerate(moves)]
    for copy in copies:
        copy.start()

    def wait_for(*which):
        def wait():
            for i in which:
                copies[i].wait()
        return wait

    base = 8 * n_col
    first_row = params[base] * tile_rows + params[base + 1] * own
    keep = (
        jnp.where(first_row > 0, 1.0, 0.0),
        jnp.where(first_row + own < n_row * tile_rows, 1.0, 0.0),
    )
    lanes = chans // 128 * 128 + 128
    bias1, bias2 = bias_ref.at[:, pl.ds(0, lanes)], bias_ref.at[:, pl.ds(lanes, lanes)]
    dc = proj.shape[1]
    part = dc // 2

    def beside(g):
        if g == 0:
            wait_for(6, 7, 8)()
        pair_part(lower, g * part, part)

    tile_body(
        geom, chans, tall, params, m1, r1, bias1, m2, r2, bias2, canvas, xm, xr, am, ar, cells_ref,
        (wait_for(0, 1), wait_for(2, 3), beside),
    )
    decoder_body(
        keep, canvas, proj, bias_ref.at[:, pl.ds(2 * lanes, dc)], bias_ref.at[:, pl.ds(2 * lanes + dc, dc)], out_hbm, out_ref, out_sems,
        hid, beyond, across, down, down_beyond, down_across, first, comps, edge, zipped, upper, lower,
        (wait_for(4), wait_for(5)),
    )


def main_call(geom, params, tall, pick, m1, r1, m2, r2, biases, proj, upper, lower, chans):
    n_row, n_col, tile_rows, tile_cols, own = geom
    width = n_col * tile_cols
    rows = own + 2
    dc = proj.shape[1]
    vm = pl.BlockSpec(memory_space=pltpu.VMEM)
    anyspace = pl.BlockSpec(memory_space=pl.ANY)

    def kernel(*refs):
        main_kernel(geom, chans, pick, *refs)

    return pl.pallas_call(
        kernel,
        out_shape=jax.ShapeDtypeStruct((2 * own, 2 * width, dc), BF),
        in_specs=[pl.BlockSpec(memory_space=pltpu.SMEM), vm] + [anyspace] * 7 + [vm] * len(tall),
        out_specs=anyspace,
        scratch_shapes=tile_scratch(geom, chans)
        + [pltpu.VMEM((rows, width, dc), BF)] * 3
        + [pltpu.VMEM((rows - 1, width, dc), BF)] * 3
        + [
            pltpu.VMEM((24, dc), F32),
            pltpu.VMEM((4, 2 * own + 2, width, dc), BF),
            pltpu.VMEM((2, width + 16, dc), F32),
            pltpu.VMEM((dc // 128, 2 * own * width, 128), F32),
            pltpu.VMEM((2 * own, 2 * width, dc), BF),
        ]
        + [pltpu.VMEM(u.shape, BF) for u in (m1, r1, m2, r2, proj, upper)]
        + [
            pltpu.VMEM((4, 3, dc, dc), BF),
            pltpu.SemaphoreType.DMA((9,)),
            pltpu.SemaphoreType.DMA((2,)),
        ],
        compiler_params=pltpu.CompilerParams(vmem_limit_bytes=VMEM_LIMIT),
        cost_estimate=pl.CostEstimate(flops=25_000_000_000, bytes_accessed=20 << 20, transcendentals=0),
    )(params, biases, m1, r1, m2, r2, proj, upper, lower, *tall)


def tile_bounds(tile_reach, row_id, col_id, n_row, n_col, tile_rows, tile_cols, own):
    first_row = row_id * tile_rows + col_id * own - HALO
    other = jnp.where(col_id < n_col // 2, row_id - 1, row_id + 1)
    bands = jnp.stack([row_id, other])
    reach = tile_reach[jnp.clip(bands, 0, n_row - 1)]
    bands = bands[:, None]
    tiles = jnp.arange(n_col, dtype=jnp.int32)[None, :]
    row_lo = jnp.maximum(bands * tile_rows - reach[:, :, 0], 0) - first_row
    row_hi = jnp.minimum((bands + 1) * tile_rows + reach[:, :, 1], n_row * tile_rows) - first_row
    row_hi = jnp.where((bands >= 0) & (bands < n_row), row_hi, 0)
    col_lo = jnp.where(tiles > 0, MARGIN - reach[:, :, 2], MARGIN)
    col_hi = jnp.where(tiles < n_col - 1, MARGIN + tile_cols + reach[:, :, 3], MARGIN + tile_cols)
    return jnp.stack([row_lo, row_hi, col_lo, col_hi]).reshape(4, 2 * n_col).astype(jnp.int32)


def swapped_rows(rows, odd, n_all):
    own = rows.shape[0]
    last = own - HALO
    between = [(i, i + 1) for i in range(1, n_all - 1, 2)]
    within = [(i, i + 1) for i in range(0, n_all, 2)]
    got = []
    for pairs, start in ((between, jnp.where(odd, last, 0)), (within, jnp.where(odd, 0, last))):
        part = lax.dynamic_slice_in_dim(rows, start, HALO, axis=0)
        got.append(lax.ppermute(part, ("row", "col"), pairs + [(b, a) for a, b in pairs]))
    return got


def halo_rows(rows, n_all):
    own = rows.shape[0]
    above, below = [], []
    left, hop = HALO, 1
    while left > 0:
        take = min(own, left)
        above.insert(0, lax.ppermute(rows[own - take :], ("row", "col"), [(i, i + hop) for i in range(n_all - hop)]))
        below.append(lax.ppermute(rows[:take], ("row", "col"), [(i + hop, i) for i in range(n_all - hop)]))
        left -= take
        hop += 1
    return above, below


def on_device(
    latent, tile_reach, first_weight, first_bias, second_weight, second_bias, proj_weight,
    upper_weight, upper_bias, lower_weight, lower_bias,
):
    chans = first_weight.shape[2]
    dc = proj_weight.shape[1]
    tile_rows = latent.shape[0]
    tile_cols = latent.shape[1] // chans
    n_row = lax.axis_size("row")
    n_col = lax.axis_size("col")
    row_id = lax.axis_index("row")
    col_id = lax.axis_index("col")
    own = tile_rows // n_col
    geom = (n_row, n_col, tile_rows, tile_cols, own)

    moved = lax.all_to_all(
        latent.reshape(n_col, own, tile_cols * chans), "col", split_axis=0, concat_axis=0
    )
    fill = jnp.zeros((-chans % 128,), F32)
    biases = jnp.concatenate([first_bias, fill, second_bias, fill, upper_bias, lower_bias]).reshape(1, -1)
    bounds = tile_bounds(tile_reach, row_id, col_id, n_row, n_col, tile_rows, tile_cols, own)
    params = jnp.concatenate([bounds.reshape(-1), jnp.stack([row_id, col_id]).astype(jnp.int32)])
    early = (params, biases, setup_call(first_weight, second_weight))
    moved, early, upper_weight = lax.optimization_barrier((moved, early, upper_weight))
    params, biases, taps = early

    rows = moved.transpose(1, 0, 2)
    if own >= HALO and n_col % 2 == 0:
        across, inside = swapped_rows(rows, lax.rem(col_id, 2) == 1, n_row * n_col)
        tall, pick = [rows, across, inside], [(2, 1), (0, 0), (1, 2)]
    else:
        above, below = halo_rows(rows, n_row * n_col)
        tall = above + [rows] + below
        pick = [(i, i) for i in range(len(tall))]
    upper = upper_call(upper_weight.reshape(9, dc, dc))
    return main_call(
        geom, params, tall, pick, *taps, biases, proj_weight, upper, lower_weight, chans,
    )


def solution(mesh):
    in_specs = (P("row", "col"), P(), P(), P(), P(), P(), P(), P(), P(), P(), P())
    out_specs = P(("row", "col"), None, None)
    return jax.shard_map(
        on_device, mesh=mesh, in_specs=in_specs, out_specs=out_specs, check_vma=False
    )
```

```python
import jax
import jax.numpy as jnp
from jax import lax
from jax.experimental import pallas as pl
from jax.experimental.pallas import tpu as pltpu
from jax.sharding import PartitionSpec as P

BF = jnp.bfloat16
F32 = jnp.float32
MARGIN = 4
HALO = 3
VMEM_LIMIT = 62 * 1024 * 1024
PAIR_ORDER = ((0, 0), (0, 1), (1, 0), (1, 1), (0, 2), (1, 2), (2, 0), (2, 1), (2, 2))


def silu(v):
    return v / (1.0 + jnp.exp(-v))


def tap_kernel(w_ref, main_ref, rest_ref):
    chans = w_ref.shape[2]
    main = chans // 128 * 128
    rest = chans - main
    depth = main_ref.shape[0] // 3
    main_ref[...] = jnp.zeros_like(main_ref)
    rest_ref[...] = jnp.zeros_like(rest_ref)
    for dy in range(3):
        for dx in range(3):
            main_ref[dy * depth + dx * main : dy * depth + dx * main + main, :] = w_ref[dy, dx, :main, :main]
            at = 3 * main + dx * rest
            main_ref[dy * depth + at : dy * depth + at + rest, :] = w_ref[dy, dx, main:, :main]
    for dx in range(3):
        for lo, n, at in ((0, main, dx * main), (main, rest, 3 * main + dx * rest)):
            tails = [w_ref[dy, dx, lo : lo + n, main:].astype(F32) for dy in range(3)]
            rest_ref[at : at + n, :128] = jnp.concatenate(tails[:2], axis=1).astype(BF)
            rest_ref[at : at + n, 128 : 128 + rest] = tails[2].astype(BF)


def setup_kernel(w1_ref, w2_ref, m1_ref, r1_ref, m2_ref, r2_ref):
    tap_kernel(w1_ref, m1_ref, r1_ref)
    tap_kernel(w2_ref, m2_ref, r2_ref)


def setup_call(w1, w2):
    chans = w1.shape[2]
    main = chans // 128 * 128
    rest = chans - main
    assert 2 * rest == 128
    depth = 3 * main + 4 * rest
    taps = [jax.ShapeDtypeStruct((3 * depth, main), BF), jax.ShapeDtypeStruct((depth, 256), BF)]
    return pl.pallas_call(
        setup_kernel,
        out_shape=taps + taps,
        compiler_params=pltpu.CompilerParams(vmem_limit_bytes=VMEM_LIMIT),
        cost_estimate=pl.CostEstimate(flops=0, bytes_accessed=8 << 20, transcendentals=0),
    )(w1, w2)


def put_cells(main_ref, rest_ref, r, v, main):
    span = v.shape[0]
    main_ref[r, pl.ds(1, span)] = v[:, :, :main].astype(BF)
    rest = v[:, :, main:]
    none = jnp.zeros((1,) + rest.shape[1:], F32)
    before = jnp.concatenate([none, rest[:-1]], axis=0)
    after = jnp.concatenate([rest[1:], none], axis=0)
    rest_ref[r, :, :, :128] = (before + pltpu.roll(rest, 64, 2)).astype(BF)
    rest_ref[r, :, :, 128:] = after.astype(BF)


def conv_group(main_ref, rest_ref, w_main, w_rest, start, rows, tail):
    span, slots = rest_ref.shape[1:3]
    main = main_ref.shape[3]
    size = rows * span * slots
    parts = []
    for dy in range(3):
        for dx in range(3):
            parts.append(main_ref[pl.ds(start + dy, rows), pl.ds(dx, span)].reshape(size, main))
        parts.append(rest_ref[pl.ds(start + dy, rows)].reshape(size, 256))
    big = jnp.dot(jnp.concatenate(parts, axis=1), w_main[...], preferred_element_type=F32)
    fresh = start + 2 if tail is not None else start
    count = rows + 2 - (fresh - start)
    size = count * span * slots
    parts = [main_ref[pl.ds(fresh, count), pl.ds(dx, span)].reshape(size, main) for dx in range(3)]
    parts.append(rest_ref[pl.ds(fresh, count)].reshape(size, 256))
    part = jnp.dot(jnp.concatenate(parts, axis=1), w_rest[...], preferred_element_type=F32)
    part = part.reshape(count, span, slots, 256)
    if tail is not None:
        part = jnp.concatenate([tail, part], axis=0)
    rest = part[:-2, :, :, :128] + pltpu.roll(part[1:-1, :, :, :128], 64, 3) + part[2:, :, :, 128:]
    return big.reshape(rows, span, slots, main), rest, part[-2:]


def tile_body(geom, chans, tall, params, m1, r1, b1_ref, m2, r2, b2_ref, canvas, xm, xr, am, ar, waits):
    n_row, n_col, tile_rows, tile_cols, own = geom
    slots = 2 * n_col
    span = tile_cols + 2 * MARGIN
    main = chans // 128 * 128
    lanes = main + 128
    rows_x = own + 2 * HALO
    width = n_col * tile_cols
    live = (lax.broadcasted_iota(jnp.int32, (1, 1, 128), 2) < chans - main).astype(F32)
    cell = lax.broadcasted_iota(jnp.int32, (span, slots, 128), 0)
    slot = lax.broadcasted_iota(jnp.int32, (slots, 128), 0)

    def per_slot(k):
        out = jnp.zeros((slots, 128), jnp.int32)
        for i in range(slots):
            out = jnp.where(slot == i, params[k * slots + i], out)
        return out

    bounds_ref = [per_slot(k) for k in range(4)]
    cols_ok = ((cell >= bounds_ref[2]) & (cell < bounds_ref[3])).astype(F32)
    xm[...] = jnp.zeros_like(xm)
    am[...] = jnp.zeros_like(am)

    def mask_of(r):
        row = jnp.zeros((slots, 128), jnp.int32) + r
        rows_ok = ((row >= bounds_ref[0]) & (row < bounds_ref[1])).astype(F32)
        return cols_ok * rows_ok

    def wide(m):
        return jnp.concatenate([m] * (lanes // 128), axis=2)

    r = 0
    is_odd = lax.rem(params[4 * slots + 1], 2) == 1
    for on_odd, on_even in tall:
        for k in range(on_odd.shape[0]):
            cols = []
            for c in range(tile_cols):
                lo = c * chans
                off = lo % 128
                at = slice(lo - off, lo - off + lanes)
                v = on_odd[k, :, at].astype(F32)
                if on_even is not on_odd:
                    v = jnp.where(is_odd, v, on_even[k, :, at].astype(F32))
                if off:
                    v = pltpu.roll(v, lanes - off, 1)
                cols.append(v)
            v = jnp.stack(cols, axis=0)
            v = jnp.concatenate([v[:, :, :main], v[:, :, main:] * live], axis=2)
            v = jnp.concatenate(
                [pltpu.roll(v[-MARGIN:], 1, 1), v, pltpu.roll(v[:MARGIN], n_col - 1, 1)], axis=0)
            v = jnp.concatenate([v, v], axis=1)
            put_cells(xm, xr, r, v * wide(mask_of(r)), main)
            r += 1

    group1 = (rows_x - 2) // 2
    def first(g, carry):
        big, rest, tail = conv_group(xm, xr, m1, r1, g * group1, group1, carry)
        for i in range(group1):
            a = g * group1 + i
            v = jnp.concatenate([big[i], rest[i] * live], axis=2) + b1_ref[...]
            put_cells(am, ar, a, silu(v) * wide(mask_of(a + 1)), main)
        return tail
    waits[0]()
    tail = None
    for g in range(2):
        tail = first(g, tail)

    group2 = (rows_x - 4) // 2
    def second(g, carry):
        waits[2](g)
        big, rest, tail = conv_group(am, ar, m2, r2, g * group2, group2, carry)
        for i in range(group2):
            a = g * group2 + i
            v = jnp.concatenate([big[i], rest[i] * live], axis=2) + b2_ref[...]
            x_rest = pltpu.roll(xr[a + 2, :, :, :128].astype(F32), 64, 2) * live
            x = jnp.concatenate([xm[a + 2, pl.ds(1, span)].astype(F32), x_rest], axis=2)
            mask = mask_of(a + 2)
            y = ((v + x) * wide(mask)).astype(BF).astype(F32)

            def fold(u):
                u = u[:, :n_col] + u[:, n_col:]
                mid = u[MARGIN:-MARGIN]
                return jnp.concatenate(
                    [
                        mid[:MARGIN] + pltpu.roll(u[-MARGIN:], 1, 1),
                        mid[MARGIN:-MARGIN],
                        mid[-MARGIN:] + pltpu.roll(u[:MARGIN], n_col - 1, 1),
                    ],
                    axis=0,
                )

            count = fold(mask)
            blend = fold(y) * wide(jnp.where(count > 0, 1.0 / jnp.maximum(count, 1.0), 0.0))
            for c in range(tile_cols):
                for lane in range(lanes // 128):
                    canvas[lane, pl.ds(a * width + c, n_col, stride=tile_cols), :] = blend[c, :, lane * 128 : lane * 128 + 128]
        return tail
    waits[1]()
    tail = None
    for g in range(2):
        tail = second(g, tail)


def tile_scratch(geom, chans):
    n_row, n_col, tile_rows, tile_cols, own = geom
    slots = 2 * n_col
    span = tile_cols + 2 * MARGIN
    main = chans // 128 * 128
    rows_x = own + 2 * HALO
    return [
        pltpu.VMEM((main // 128 + 1, (own + 2) * n_col * tile_cols, 128), F32),
        pltpu.VMEM((rows_x, span + 2, slots, main), BF),
        pltpu.VMEM((rows_x, span, slots, 256), BF),
        pltpu.VMEM((rows_x - 2, span + 2, slots, main), BF),
        pltpu.VMEM((rows_x - 2, span, slots, 256), BF),
    ]


def halves(first, second, third):
    half = 0.5 * second
    return first + half, third + half, half


def upper_kernel(w_hbm, out_hbm, w_ref, out_ref, in_sems, out_sems):
    step = w_ref.shape[1] // 4
    parts = [pl.ds(i * step, step) for i in range(4)]
    reads = [pltpu.make_async_copy(w_hbm.at[:, at], w_ref.at[:, at], in_sems.at[i]) for i, at in enumerate(parts)]
    writes = [pltpu.make_async_copy(out_ref.at[:, at], out_hbm.at[:, at], out_sems.at[i]) for i, at in enumerate(parts)]
    for read in reads:
        read.start()
    for read, write, at in zip(reads, writes, parts):
        read.wait()
        w = [[w_ref[3 * dy + dx, at, :].astype(F32) for dx in range(3)] for dy in range(3)]
        rows = [halves(w[0][dx], w[1][dx], w[2][dx]) for dx in range(3)]
        both = [halves(rows[0][r], rows[1][r], rows[2][r]) for r in range(3)]
        for i, (r, c) in enumerate(PAIR_ORDER):
            out_ref[i, at, :] = both[r][c].astype(BF)
        write.start()
    for write in writes:
        write.wait()


def upper_call(w):
    anyspace = pl.BlockSpec(memory_space=pl.ANY)
    return pl.pallas_call(
        upper_kernel,
        out_shape=jax.ShapeDtypeStruct(w.shape, BF),
        in_specs=[anyspace],
        out_specs=anyspace,
        scratch_shapes=[pltpu.VMEM(w.shape, BF)] * 2 + [pltpu.SemaphoreType.DMA((4,))] * 2,
        compiler_params=pltpu.CompilerParams(vmem_limit_bytes=VMEM_LIMIT),
        cost_estimate=pl.CostEstimate(flops=0, bytes_accessed=4 * w.size, transcendentals=0),
    )(w)


def pair_part(w, k0, kn):
    ks = pl.ds(k0, kn)
    for dy in range(3):
        ends = 0.5 * (w[0, dy, ks, :].astype(F32) + w[3, dy, ks, :].astype(F32))
        mid = 0.5 * w[1, dy, ks, :].astype(F32)
        w[1, dy, ks, :] = (ends + mid).astype(BF)
        w[2, dy, ks, :] = (ends - mid).astype(BF)


def decoder_body(
    keep, canvas, proj_ref, ub_ref, lb_ref, out_hbm, out_ref, out_sems, hid, beyond, across, down, down_beyond,
    down_across, first, comps, edge, zipped, upper_v, lower_v, waits,
):
    rows, width, dc = hid.shape
    steps = rows - 1
    own = rows - 2
    chans = proj_ref.shape[0]
    main = chans // 128 * 128

    edge[...] = jnp.zeros_like(edge)
    first[...] = jnp.zeros_like(first)
    waits[0]()
    last = None
    for r in range(rows):
        at = pl.ds(r * width, width)
        x = jnp.concatenate([canvas[lane, at, :] for lane in range(main // 128)], axis=1).astype(BF)
        rest = canvas[main // 128, at, :].astype(BF)[:, : chans - main]
        h = jnp.dot(x, proj_ref[:main, :], preferred_element_type=F32)
        h = h + jnp.dot(rest, proj_ref[main:, :], preferred_element_type=F32)
        h = h.astype(BF)
        hid[r] = h
        h = h.astype(F32)
        edge[0, pl.ds(8, width), :] = h
        first[pl.ds(r, 1), :] = h[:1]
        b = edge[0, pl.ds(9, width), :]
        beyond[r] = b.astype(BF)
        across[r] = (h - b).astype(BF)
        if last is not None:
            down[r - 1] = (last[0] - h).astype(BF)
            down_beyond[r - 1] = (last[1] - b).astype(BF)
            down_across[r - 1] = ((last[0] - h) - (last[1] - b)).astype(BF)
        last = (h, b)

    waits[1]()
    near, far = first[pl.ds(0, 16), :], first[pl.ds(1, 16), :]
    none = jnp.zeros((16, dc), BF)

    def side(ref, start, extra):
        return jnp.concatenate([ref[pl.ds(start, steps)].reshape(steps * width, dc), extra.astype(BF)], axis=0)

    def product(parts, at):
        rhs = upper_v[pl.ds(at, len(parts))].reshape(len(parts) * dc, dc)
        return jnp.dot(jnp.concatenate(parts, axis=1), rhs, preferred_element_type=F32)

    sums = product([side(hid, 0, none), side(beyond, 0, near), side(hid, 1, none), side(beyond, 1, far)], 0)
    cols = product([side(across, 0, -near), side(across, 1, -far)], 4)
    lines = product([side(down, 0, none), side(down_beyond, 0, near - far)], 6)
    cross = product([side(down_across, 0, far - near)], 8)
    col_id = lax.broadcasted_iota(jnp.int32, (width, 1), 0)
    for p in (1, 0):
        if p == 1:
            straight, turned = sums + lines, cols + cross
        else:
            straight, turned = sums - lines, cols - cross
        odd = silu(straight + turned + ub_ref[...])
        even = silu(straight - turned + ub_ref[...])
        for k in range(steps):
            scale = 1.0
            if k == 0 and p == 1:
                scale = keep[0]
            if k == steps - 1 and p == 0:
                scale = keep[1]
            o = (odd[k * width : (k + 1) * width] * scale).astype(BF).astype(F32)
            after = (even[k * width : (k + 1) * width] * scale).astype(BF).astype(F32)
            after = jnp.where(col_id < width - 1, after, 0.0)
            start = (even[steps * width + k : steps * width + k + 1] * scale).astype(BF).astype(F32)
            edge[0, pl.ds(8, width), :] = o
            edge[1, pl.ds(8, width), :] = after
            edge[1, pl.ds(7, 1), :] = start
            e = edge[1, pl.ds(7, width), :]
            at = 2 * k + 1 - p
            comps[0, at] = (edge[0, pl.ds(7, width), :] - o).astype(BF)
            comps[1, at] = (e + o).astype(BF)
            comps[2, at] = (o - e).astype(BF)
            comps[3, at] = (e - after).astype(BF)

    group = own
    copies = []
    for n in range(2 * own // group):
        start = n * group
        prods = []
        for i in range(4):
            lhs = jnp.concatenate(
                [comps[i, pl.ds(start + dy, group)].reshape(group * width, dc) for dy in range(3)], axis=1)
            prods.append(jnp.dot(lhs, lower_v[i].reshape(3 * dc, dc), preferred_element_type=F32))
        both = (prods[0] + (prods[1] + prods[2]), (prods[1] - prods[2]) - prods[3])
        for g in range(group):
            base = hid[1 + (start + g) // 2].astype(F32) + lb_ref[...]
            for q in range(2):
                v = both[q][g * width : (g + 1) * width] + base
                for lane in range(dc // 128):
                    zipped[lane, pl.ds(g * 2 * width + q, width, stride=2), :] = v[:, lane * 128 : lane * 128 + 128]
            for lane in range(dc // 128):
                out_ref[start + g, :, pl.ds(lane * 128, 128)] = zipped[lane, pl.ds(g * 2 * width, 2 * width), :].astype(BF)
            copy = pltpu.make_async_copy(out_ref.at[start + g], out_hbm.at[start + g], out_sems.at[start + g])
            copy.start()
            copies.append(copy)
    for copy in copies:
        copy.wait()


def main_kernel(geom, chans, pick, params, bias_ref, *refs):
    n_row, n_col, tile_rows, tile_cols, own = geom
    m1_in, r1_in, m2_in, r2_in, proj_in, upper_in, lower_in = refs[:7]
    n_tall = 1 + max(max(p) for p in pick)
    tall = [(refs[7 + a], refs[7 + b]) for a, b in pick]
    refs = refs[7 + n_tall :]
    (out_hbm, canvas, xm, xr, am, ar, hid, beyond, across, down, down_beyond, down_across, first, comps,
     edge, zipped, out_ref, m1, r1, m2, r2, proj, upper, lower, sems, out_sems) = refs
    moves = [
        (m1_in, m1), (r1_in, r1), (m2_in, m2), (r2_in, r2), (proj_in, proj), (upper_in, upper),
        (lower_in.at[:, 0], lower.at[0]), (lower_in.at[:, 1], lower.at[1]), (lower_in.at[:, 2], lower.at[3]),
    ]
    copies = [pltpu.make_async_copy(src, dst, sems.at[i]) for i, (src, dst) in enumerate(moves)]
    for copy in copies:
        copy.start()

    def wait_for(*which):
        def wait():
            for i in which:
                copies[i].wait()
        return wait

    base = 8 * n_col
    first_row = params[base] * tile_rows + params[base + 1] * own
    keep = (
        jnp.where(first_row > 0, 1.0, 0.0),
        jnp.where(first_row + own < n_row * tile_rows, 1.0, 0.0),
    )
    lanes = chans // 128 * 128 + 128
    bias1, bias2 = bias_ref.at[:, pl.ds(0, lanes)], bias_ref.at[:, pl.ds(lanes, lanes)]
    dc = proj.shape[1]
    part = dc // 2

    def beside(g):
        if g == 0:
            wait_for(6, 7, 8)()
        pair_part(lower, g * part, part)

    tile_body(
        geom, chans, tall, params, m1, r1, bias1, m2, r2, bias2, canvas, xm, xr, am, ar,
        (wait_for(0, 1), wait_for(2, 3), beside),
    )
    decoder_body(
        keep, canvas, proj, bias_ref.at[:, pl.ds(2 * lanes, dc)], bias_ref.at[:, pl.ds(2 * lanes + dc, dc)], out_hbm, out_ref, out_sems,
        hid, beyond, across, down, down_beyond, down_across, first, comps, edge, zipped, upper, lower,
        (wait_for(4), wait_for(5)),
    )


def main_call(geom, params, tall, pick, m1, r1, m2, r2, biases, proj, upper, lower, chans):
    n_row, n_col, tile_rows, tile_cols, own = geom
    width = n_col * tile_cols
    rows = own + 2
    dc = proj.shape[1]
    vm = pl.BlockSpec(memory_space=pltpu.VMEM)
    anyspace = pl.BlockSpec(memory_space=pl.ANY)

    def kernel(*refs):
        main_kernel(geom, chans, pick, *refs)

    return pl.pallas_call(
        kernel,
        out_shape=jax.ShapeDtypeStruct((2 * own, 2 * width, dc), BF),
        in_specs=[pl.BlockSpec(memory_space=pltpu.SMEM), vm] + [anyspace] * 7 + [vm] * len(tall),
        out_specs=anyspace,
        scratch_shapes=tile_scratch(geom, chans)
        + [pltpu.VMEM((rows, width, dc), BF)] * 3
        + [pltpu.VMEM((rows - 1, width, dc), BF)] * 3
        + [
            pltpu.VMEM((24, dc), F32),
            pltpu.VMEM((4, 2 * own + 2, width, dc), BF),
            pltpu.VMEM((2, width + 16, dc), F32),
            pltpu.VMEM((dc // 128, 2 * own * width, 128), F32),
            pltpu.VMEM((2 * own, 2 * width, dc), BF),
        ]
        + [pltpu.VMEM(u.shape, BF) for u in (m1, r1, m2, r2, proj, upper)]
        + [
            pltpu.VMEM((4, 3, dc, dc), BF),
            pltpu.SemaphoreType.DMA((9,)),
            pltpu.SemaphoreType.DMA((2 * own,)),
        ],
        compiler_params=pltpu.CompilerParams(vmem_limit_bytes=VMEM_LIMIT),
        cost_estimate=pl.CostEstimate(flops=25_000_000_000, bytes_accessed=20 << 20, transcendentals=0),
    )(params, biases, m1, r1, m2, r2, proj, upper, lower, *tall)


def tile_bounds(tile_reach, row_id, col_id, n_row, n_col, tile_rows, tile_cols, own):
    first_row = row_id * tile_rows + col_id * own - HALO
    other = jnp.where(col_id < n_col // 2, row_id - 1, row_id + 1)
    bands = jnp.stack([row_id, other])
    reach = tile_reach[jnp.clip(bands, 0, n_row - 1)]
    bands = bands[:, None]
    tiles = jnp.arange(n_col, dtype=jnp.int32)[None, :]
    row_lo = jnp.maximum(bands * tile_rows - reach[:, :, 0], 0) - first_row
    row_hi = jnp.minimum((bands + 1) * tile_rows + reach[:, :, 1], n_row * tile_rows) - first_row
    row_hi = jnp.where((bands >= 0) & (bands < n_row), row_hi, 0)
    col_lo = jnp.where(tiles > 0, MARGIN - reach[:, :, 2], MARGIN)
    col_hi = jnp.where(tiles < n_col - 1, MARGIN + tile_cols + reach[:, :, 3], MARGIN + tile_cols)
    return jnp.stack([row_lo, row_hi, col_lo, col_hi]).reshape(4, 2 * n_col).astype(jnp.int32)


def swapped_rows(rows, odd, n_all):
    own = rows.shape[0]
    last = own - HALO
    between = [(i, i + 1) for i in range(1, n_all - 1, 2)]
    within = [(i, i + 1) for i in range(0, n_all, 2)]
    got = []
    for pairs, start in ((between, jnp.where(odd, last, 0)), (within, jnp.where(odd, 0, last))):
        part = lax.dynamic_slice_in_dim(rows, start, HALO, axis=0)
        got.append(lax.ppermute(part, ("row", "col"), pairs + [(b, a) for a, b in pairs]))
    return got


def halo_rows(rows, n_all):
    own = rows.shape[0]
    above, below = [], []
    left, hop = HALO, 1
    while left > 0:
        take = min(own, left)
        above.insert(0, lax.ppermute(rows[own - take :], ("row", "col"), [(i, i + hop) for i in range(n_all - hop)]))
        below.append(lax.ppermute(rows[:take], ("row", "col"), [(i + hop, i) for i in range(n_all - hop)]))
        left -= take
        hop += 1
    return above, below


def on_device(
    latent, tile_reach, first_weight, first_bias, second_weight, second_bias, proj_weight,
    upper_weight, upper_bias, lower_weight, lower_bias,
):
    chans = first_weight.shape[2]
    dc = proj_weight.shape[1]
    tile_rows = latent.shape[0]
    tile_cols = latent.shape[1] // chans
    n_row = lax.axis_size("row")
    n_col = lax.axis_size("col")
    row_id = lax.axis_index("row")
    col_id = lax.axis_index("col")
    own = tile_rows // n_col
    geom = (n_row, n_col, tile_rows, tile_cols, own)

    moved = lax.all_to_all(
        latent.reshape(n_col, own, tile_cols * chans), "col", split_axis=0, concat_axis=0
    )
    fill = jnp.zeros((-chans % 128,), F32)
    biases = jnp.concatenate([first_bias, fill, second_bias, fill, upper_bias, lower_bias]).reshape(1, -1)
    bounds = tile_bounds(tile_reach, row_id, col_id, n_row, n_col, tile_rows, tile_cols, own)
    params = jnp.concatenate([bounds.reshape(-1), jnp.stack([row_id, col_id]).astype(jnp.int32)])
    early = (params, biases, setup_call(first_weight, second_weight))
    moved, early, upper_weight = lax.optimization_barrier((moved, early, upper_weight))
    params, biases, taps = early

    rows = moved.transpose(1, 0, 2)
    if own >= HALO and n_col % 2 == 0:
        across, inside = swapped_rows(rows, lax.rem(col_id, 2) == 1, n_row * n_col)
        tall, pick = [rows, across, inside], [(2, 1), (0, 0), (1, 2)]
    else:
        above, below = halo_rows(rows, n_row * n_col)
        tall = above + [rows] + below
        pick = [(i, i) for i in range(len(tall))]
    upper = upper_call(upper_weight.reshape(9, dc, dc))
    return main_call(
        geom, params, tall, pick, *taps, biases, proj_weight, upper, lower_weight, chans,
    )


def solution(mesh):
    in_specs = (P("row", "col"), P(), P(), P(), P(), P(), P(), P(), P(), P(), P())
    out_specs = P(("row", "col"), None, None)
    return jax.shard_map(
        on_device, mesh=mesh, in_specs=in_specs, out_specs=out_specs, check_vma=False
    )
```
